32 devices in a mesh: dp: 8 (over y, x, core), tensor: 4 (over z).
Axes of the slice: x: 2, y: 2, z: 4, core: 2. Of those that a mesh axis runs over, the one named last changes fastest.
Arguments:
- activations: bfloat16 [8192, 5120], P('dp', 'tensor'), may hold values from -36 to 36, as said below
- out_grads: bfloat16 [8192, 4096], P('dp', 'tensor'), may hold values from -0.04375 to 0.04375, as said below
Outputs:
- combined: float32 [5120, 4096], P('dp', 'tensor')
The draws below stay inside these ranges and needn't reach their ends.
Inputs may be any that keep to these rules, and one draw needn't show every extreme that they name: Replicas' activations share a common part and features have different scales. `out_grads`: Replicas' output gradients share a common part and columns have different scales.
All inputs are finite; a program needn't handle non-finite values.
Results may differ from the reference program's by a relative error of at most 0.0003.
Values may be sent and summed in bfloat16 or wider, within the bound.
A program may use at most 128 MiB of HBM per device.

```python
import math
import jax
import jax.numpy as jnp

D = 5120
F = 4096
TOK_DEV = 1024
REPLICAS = 8


def assemble(common_part, own_part, common_weight, own_weight, top_scale, feature_scale, overall):
    ladder = 1.0 + (top_scale - 1.0) * jnp.arange(REPLICAS, dtype=jnp.float32) / max(REPLICAS - 1, 1)
    mixed = common_weight * common_part[None] + own_weight * own_part
    mixed = mixed * ladder[:, None, None] * feature_scale[None, None, :] * overall
    return mixed.reshape(REPLICAS * common_part.shape[0], common_part.shape[1])


def draw_activations(key, part):
    key = jax.random.fold_in(key, 11)
    key_common, key_own, key_scale = jax.random.split(key, 3)
    feature_scale = jnp.exp(jax.random.uniform(key_scale, (D,), jnp.float32, -0.5 * math.log(10.0), 0.5 * math.log(10.0)))
    common_part = jax.random.normal(key_common, (TOK_DEV, D), jnp.float32)
    own_part = jax.random.normal(key_own, (REPLICAS, TOK_DEV, D), jnp.float32)
    result = assemble(common_part, own_part, 0.8, 0.6, 3.0, feature_scale, 1.0)
    return jnp.clip(result, -36.0, 36.0).astype(jnp.bfloat16)


def draw_out_grads(key, part):
    key = jax.random.fold_in(key, 23)
    key_common, key_own, key_scale = jax.random.split(key, 3)
    feature_scale = jnp.exp(jax.random.uniform(key_scale, (F,), jnp.float32, -0.5 * math.log(10.0), 0.5 * math.log(10.0)))
    overall = 0.2 / math.sqrt(TOK_DEV)
    limit = 1.4 / math.sqrt(TOK_DEV)
    common_part = jax.random.normal(key_common, (TOK_DEV, F), jnp.float32)
    own_part = jax.random.normal(key_own, (REPLICAS, TOK_DEV, F), jnp.float32)
    result = assemble(common_part, own_part, 0.8, 0.6, 1.0, feature_scale, overall)
    return jnp.clip(result, -limit, limit).astype(jnp.bfloat16)


def setup_inputs(seed: int = 0) -> dict:
    key_list = jax.random.split(jax.random.key(seed), 3)
    activations = draw_activations(jax.random.fold_in(key_list[2], 71), 0)
    out_grads = draw_out_grads(jax.random.fold_in(key_list[2], 71), 0)
    return dict(activations=activations, out_grads=out_grads)


epsilon = 1e-06

def adasum(left, right):
    cross_dot = jnp.sum(left * right)
    left_norm = jnp.sum(left * left)
    right_norm = jnp.sum(right * right)
    return (1.0 - cross_dot / (2.0 * (left_norm + epsilon))) * left + (1.0 - cross_dot / (2.0 * (right_norm + epsilon))) * right

def reference(activations, out_grads):

    def replica_grad(replica_index):
        rows_x = activations[replica_index * TOK_DEV:(replica_index + 1) * TOK_DEV]
        grad_rows = out_grads[replica_index * TOK_DEV:(replica_index + 1) * TOK_DEV]
        return jnp.dot(rows_x.T, grad_rows, preferred_element_type=jnp.float32)

    def combined_tree(lower_index, members):
        if members == 1:
            return replica_grad(lower_index)
        half_count = members // 2
        return adasum(combined_tree(lower_index, half_count), combined_tree(lower_index + half_count, half_count))
    return combined_tree(0, REPLICAS)
```

```python
import functools
import jax
import jax.numpy as jnp
from jax import lax
from jax.experimental import pallas as pl
from jax.experimental.pallas import tpu as pltpu
from jax.sharding import PartitionSpec as P

epsilon = 1e-06
MESH = pl.DeviceIdType.MESH
CHUNKS = 4


def swapped(x, axis, apart):
    return lax.ppermute(x, axis, [(i, i ^ 1 << apart) for i in range(lax.axis_size(axis))])


def group_totals(partials, section):
    for bit_number in range(section + 1):
        partials = partials + swapped(partials, "dp", bit_number)
    return lax.psum(partials, "tensor")


def adasum_pair(mine, other, section, replica):
    upper_side = jnp.right_shift(replica, section) % 2 == 1
    mine_norm = jnp.sum(mine * mine)
    other_norm = jnp.sum(other * other)
    lower_norm = jnp.where(upper_side, other_norm, mine_norm)
    upper_norm = jnp.where(upper_side, mine_norm, other_norm)
    partials = jnp.stack([jnp.sum(mine * other), lower_norm, upper_norm])
    totals = group_totals(partials, section)
    lower_coef = 1.0 - totals[0] / (2.0 * (totals[1] + epsilon))
    upper_coef = 1.0 - totals[0] / (2.0 * (totals[2] + epsilon))
    mine_coef = jnp.where(upper_side, upper_coef, lower_coef)
    other_coef = jnp.where(upper_side, lower_coef, upper_coef)
    return mine_coef * mine + other_coef * other


def by_halving(activations, out_grads):
    replicas = lax.axis_size("dp")
    section_count = replicas.bit_length() - 1
    replica = lax.axis_index("dp")
    columns = out_grads.shape[1]
    slab_rows = activations.shape[1]
    block_rows = slab_rows * lax.axis_size("tensor") // replicas
    full_grad = jnp.einsum(
        "tk,tf->kf",
        lax.all_gather(activations, "tensor", axis=1, tiled=True),
        out_grads,
        preferred_element_type=jnp.float32,
    )
    holding = full_grad.reshape(replicas, block_rows, columns)
    for section in range(section_count):
        section_bit = jnp.right_shift(replica, section) % 2
        paired = holding.reshape(-1, 2, block_rows, columns)
        keeping = lax.dynamic_index_in_dim(paired, section_bit, axis=1, keepdims=False)
        sending = lax.dynamic_index_in_dim(paired, 1 - section_bit, axis=1, keepdims=False)
        received = swapped(sending, "dp", section)
        holding = adasum_pair(keeping, received, section, replica)
    return holding.reshape(block_rows, columns)


def pair_list(count):
    return [(a, b) for a in range(count) for b in range(a, count)]


def tree_weights(gram, count):
    weights = [[(r, None)] for r in range(count)]
    while count > 1:
        half = count // 2
        low, high = [], []
        for i in range(half):
            aa, bb, ab = gram[2 * i, 2 * i], gram[2 * i + 1, 2 * i + 1], gram[2 * i, 2 * i + 1]
            bound = jnp.sqrt(aa) * jnp.sqrt(bb)
            ab = jnp.clip(ab, -bound, bound)
            low.append(1.0 - ab / (2.0 * (aa + epsilon)))
            high.append(1.0 - ab / (2.0 * (bb + epsilon)))
        merged = {}
        for i, j in pair_list(half):
            cross = gram[2 * i, 2 * j + 1]
            back = gram[2 * i + 1, 2 * j] if i != j else cross
            value = (
                low[i] * (low[j] * gram[2 * i, 2 * j] + high[j] * cross)
                + high[i] * (low[j] * back + high[j] * gram[2 * i + 1, 2 * j + 1])
            )
            merged[i, j] = jnp.maximum(value, 0.0) if i == j else value
        weights = [
            [(r, low[i] if w is None else w * low[i]) for r, w in weights[2 * i]]
            + [(r, high[i] if w is None else w * high[i]) for r, w in weights[2 * i + 1]]
            for i in range(half)
        ]
        gram, count = merged, half
    return [w for _, w in sorted(weights[0], key=lambda item: item[0])]


def kernel(
    R, Z, x_ref, y_ref, out_ref, fw,
    xg, yg, grads, part, first, second,
    zsend, zrecv, xsend, xrecv, ysend, yrecv, fsend, lsem, asend, arecv, bsend, brecv,
):
    me = lax.axis_index("dp")
    z = lax.axis_index("tensor")
    chips = R // 2
    chip, core = me // 2, me % 2
    sibling = chip * 2 + 1 - core
    rows = x_ref.shape[0] // CHUNKS
    width = xg.shape[2]
    columns = yg.shape[2]

    barrier = pltpu.get_barrier_semaphore()
    for j in range(1, Z):
        pl.semaphore_signal(barrier, inc=1, device_id=(me, (z + j) % Z), device_id_type=MESH)
    for j in range(1, R):
        pl.semaphore_signal(barrier, inc=1, device_id=((me + j) % R, z), device_id_type=MESH)
    pl.semaphore_wait(barrier, Z + R - 2)

    def remote(src, dst, send, recv, device):
        return pltpu.make_async_remote_copy(
            src_ref=src, dst_ref=dst, send_sem=send, recv_sem=recv,
            device_id=device, device_id_type=MESH,
        )

    def span(i):
        return pl.ds(pl.multiple_of(i * rows, rows), rows)

    def z_copy(src, s, i, way):
        to = z + 1 if way == 0 else z - 1
        return remote(
            src, fw.at[s, span(i)], zsend.at[way, s, i], zrecv.at[s, i], (me, to)
        )

    def own(i):
        return x_ref.at[span(i)]

    def held(s, i):
        return fw.at[s, span(i)]

    def scatter(src, s, i, start):
        for h in range(2):
            dest = 2 * s + h
            piece = src.at[:, pl.ds(h * width, width)]

            @pl.when(dest == me)
            def _():
                if start:
                    pltpu.make_async_copy(piece, xg.at[me, span(i)], xrecv.at[me, i]).start()

            @pl.when(dest != me)
            def _():
                copy = remote(
                    piece, xg.at[me, span(i)], xsend.at[s, i, h], xrecv.at[me, i], (dest, z)
                )
                if start:
                    copy.start()
                else:
                    copy.wait_send()

    def move_along(start):
        @pl.loop(0, CHUNKS)
        def _(i):
            for way, there in ((0, z < Z - 1), (1, z > 0)):
                @pl.when(there)
                def _():
                    copy = z_copy(own(i), z, i, way)
                    if start:
                        copy.start()
                    else:
                        copy.wait_send()
            scatter(own(i), z, i, start)

        if start:
            send_out_grads()

        for t in range(1, Z):
            @pl.loop(0, CHUNKS)
            def _(i):
                for way, s, exists, further in (
                    (0, z - t, z - t >= 0, z < Z - 1),
                    (1, z + t, z + t < Z, z > 0),
                ):
                    @pl.when(exists)
                    def _():
                        if start:
                            z_copy(held(s, i), s, i, way).wait_recv()

                        @pl.when(further)
                        def _():
                            copy = z_copy(held(s, i), s, i, way)
                            if start:
                                copy.start()
                            else:
                                copy.wait_send()
                        scatter(held(s, i), s, i, start)

            if start and t == Z - 2:
                share_out_grads()

    def y_copy(j):
        return remote(
            y_ref, yg.at[me], ysend.at[j], yrecv.at[me], (((chip + j) % chips) * 2 + core, z)
        )

    def sibling_copy():
        return remote(y_ref, yg.at[me], ysend.at[0], yrecv.at[me], (sibling, z))

    def share_copy(j):
        r = ((chip + j) % chips) * 2 + core
        return remote(yg.at[r], yg.at[r], fsend.at[j], yrecv.at[r], (sibling, z))

    def local_y():
        return pltpu.make_async_copy(y_ref, yg.at[me], lsem)

    def send_out_grads():
        for j in range(1, chips):
            y_copy(j).start()
        sibling_copy().start()
        local_y().start()

    def share_out_grads():
        for j in range(1, chips):
            r = ((chip + j) % chips) * 2 + core
            remote(yg.at[r], yg.at[r], fsend.at[j], yrecv.at[r], (sibling, z)).wait_recv()
            share_copy(j).start()

    move_along(True)

    local_y().wait()
    for j in range(chips):
        r = ((chip + j) % chips) * 2 + 1 - core
        remote(yg.at[r], yg.at[r], fsend.at[j], yrecv.at[r], (sibling, z)).wait_recv()

    tile = 256

    @pl.loop(0, CHUNKS)
    def _(i):
        @pl.loop(0, R)
        def _(r):
            pltpu.make_async_copy(xg.at[r, span(i)], xg.at[r, span(i)], xrecv.at[r, i]).wait()

            @pl.loop(0, columns // tile)
            def _(q):
                at = pl.ds(pl.multiple_of(q * tile, tile), tile)
                product = lax.dot_general(
                    xg[r, span(i), :], yg[r, span(i), at], (((0,), (0,)), ((), ())),
                    preferred_element_type=jnp.float32,
                )

                @pl.when(i == 0)
                def _():
                    grads[r, :, at] = product

                @pl.when(i > 0)
                def _():
                    grads[r, :, at] += product

    pairs = pair_list(R)

    def accumulate(b, sums):
        at = pl.ds(pl.multiple_of(b * 8, 8), 8)
        sums = list(sums)
        for q in range(columns // 128):
            blocks = [grads[r, at, pl.ds(q * 128, 128)] for r in range(R)]
            for n, (a, c) in enumerate(pairs):
                sums[n] = sums[n] + blocks[a] * blocks[c]
        return tuple(sums)

    sums = lax.fori_loop(
        0, width // 8, accumulate, tuple(jnp.zeros((8, 128), jnp.float32) for _ in pairs)
    )
    part[0] = jnp.zeros(part.shape[1:], jnp.float32)
    for n in range(len(pairs)):
        part[0, pl.ds(n, 1), :] = jnp.sum(sums[n], axis=0, keepdims=True)

    def around_z(j):
        return remote(part.at[0], first.at[j - 1], asend.at[j - 1], arecv.at[j - 1], (me, (z + j) % Z))

    def around_plane(j):
        return remote(
            part.at[1], second.at[j - 1], bsend.at[j - 1], brecv.at[j - 1], ((me + j) % R, z)
        )

    for j in range(1, Z):
        around_z(j).start()
    for j in range(1, Z):
        around_z(j).wait_recv()
    part[1] = part[0] + sum(first[j - 1] for j in range(1, Z))
    for j in range(1, R):
        around_plane(j).start()
    for j in range(1, R):
        around_plane(j).wait_recv()
    totals = part[1] + sum(second[j - 1] for j in range(1, R))
    totals = jnp.sum(totals, axis=1, keepdims=True)
    gram = {pair: totals[n:n + 1, :] for n, pair in enumerate(pairs)}
    weights = tree_weights(gram, R)

    band = 16

    @pl.loop(0, width // band)
    def _(b):
        at = pl.ds(pl.multiple_of(b * band, band), band)
        total = weights[0] * grads[0, at, :]
        for r in range(1, R):
            total = total + weights[r] * grads[r, at, :]
        out_ref[at, :] = total

    move_along(False)
    for j in range(1, chips):
        y_copy(j).wait_send()
        share_copy(j).wait_send()
    sibling_copy().wait_send()
    for j in range(1, Z):
        around_z(j).wait_send()
    for j in range(1, R):
        around_plane(j).wait_send()


def by_tiles(R, Z, activations, out_grads):
    tokens, slab = activations.shape
    columns = out_grads.shape[1]
    width = slab * Z // R
    kept = -(-len(pair_list(R)) // 8) * 8
    dma = pltpu.SemaphoreType.DMA
    return pl.pallas_call(
        functools.partial(kernel, R, Z),
        out_shape=(
            jax.ShapeDtypeStruct((width, columns), jnp.float32),
            jax.ShapeDtypeStruct((Z, tokens, slab), jnp.bfloat16),
        ),
        in_specs=[pl.BlockSpec(memory_space=pl.ANY)] * 2,
        out_specs=(
            pl.BlockSpec(memory_space=pltpu.VMEM),
            pl.BlockSpec(memory_space=pl.ANY),
        ),
        scratch_shapes=[
            pltpu.VMEM((R, tokens, width), jnp.bfloat16),
            pltpu.VMEM((R, tokens, columns), jnp.bfloat16),
            pltpu.VMEM((R, width, columns), jnp.float32),
            pltpu.VMEM((2, kept, 128), jnp.float32),
            pltpu.VMEM((Z - 1, kept, 128), jnp.float32),
            pltpu.VMEM((R - 1, kept, 128), jnp.float32),
            dma((2, Z, CHUNKS)),
            dma((Z, CHUNKS)),
            dma((Z, CHUNKS, 2)),
            dma((R, CHUNKS)),
            dma((R // 2,)),
            dma((R,)),
            dma((R // 2,)),
            dma,
            dma((Z - 1,)),
            dma((Z - 1,)),
            dma((R - 1,)),
            dma((R - 1,)),
        ],
        compiler_params=pltpu.CompilerParams(
            collective_id=0, has_side_effects=True, vmem_limit_bytes=60 * 1024 * 1024
        ),
        cost_estimate=pl.CostEstimate(
            flops=2 * R * tokens * width * columns,
            bytes_accessed=2 * R * tokens * (width + columns),
            transcendentals=0,
        ),
    )(activations, out_grads)[0]


def solution(mesh):
    R, Z = mesh.shape["dp"], mesh.shape["tensor"]

    def on_device(activations, out_grads):
        tokens, slab = activations.shape
        columns = out_grads.shape[1]
        width = slab * Z // R
        fits = (
            R == 2 * Z and R <= 8 and width % 128 == 0 and columns % 256 == 0
            and tokens % (CHUNKS * 16) == 0
            and R * (2 * tokens * (width + columns) + 4 * width * columns) < 50 * 2**20
        )
        if fits:
            return by_tiles(R, Z, activations, out_grads)
        return by_halving(activations, out_grads)

    return jax.shard_map(
        on_device,
        mesh=mesh,
        in_specs=(P("dp", "tensor"), P("dp", "tensor")),
        out_specs=P("dp", "tensor"),
        check_vma=False,
    )
```

```python
import functools
import jax
import jax.numpy as jnp
from jax import lax
from jax.experimental import pallas as pl
from jax.experimental.pallas import tpu as pltpu
from jax.sharding import PartitionSpec as P

epsilon = 1e-06
MESH = pl.DeviceIdType.MESH
CHUNKS = 8
FOLD = 2


def swapped(x, axis, apart):
    return lax.ppermute(x, axis, [(i, i ^ 1 << apart) for i in range(lax.axis_size(axis))])


def group_totals(partials, section):
    for bit_number in range(section + 1):
        partials = partials + swapped(partials, "dp", bit_number)
    return lax.psum(partials, "tensor")


def adasum_pair(mine, other, section, replica):
    upper_side = jnp.right_shift(replica, section) % 2 == 1
    mine_norm = jnp.sum(mine * mine)
    other_norm = jnp.sum(other * other)
    lower_norm = jnp.where(upper_side, other_norm, mine_norm)
    upper_norm = jnp.where(upper_side, mine_norm, other_norm)
    partials = jnp.stack([jnp.sum(mine * other), lower_norm, upper_norm])
    totals = group_totals(partials, section)
    lower_coef = 1.0 - totals[0] / (2.0 * (totals[1] + epsilon))
    upper_coef = 1.0 - totals[0] / (2.0 * (totals[2] + epsilon))
    mine_coef = jnp.where(upper_side, upper_coef, lower_coef)
    other_coef = jnp.where(upper_side, lower_coef, upper_coef)
    return mine_coef * mine + other_coef * other


def by_halving(activations, out_grads):
    replicas = lax.axis_size("dp")
    section_count = replicas.bit_length() - 1
    replica = lax.axis_index("dp")
    columns = out_grads.shape[1]
    slab_rows = activations.shape[1]
    block_rows = slab_rows * lax.axis_size("tensor") // replicas
    full_grad = jnp.einsum(
        "tk,tf->kf",
        lax.all_gather(activations, "tensor", axis=1, tiled=True),
        out_grads,
        preferred_element_type=jnp.float32,
    )
    holding = full_grad.reshape(replicas, block_rows, columns)
    for section in range(section_count):
        section_bit = jnp.right_shift(replica, section) % 2
        paired = holding.reshape(-1, 2, block_rows, columns)
        keeping = lax.dynamic_index_in_dim(paired, section_bit, axis=1, keepdims=False)
        sending = lax.dynamic_index_in_dim(paired, 1 - section_bit, axis=1, keepdims=False)
        received = swapped(sending, "dp", section)
        holding = adasum_pair(keeping, received, section, replica)
    return holding.reshape(block_rows, columns)


def pair_list(count):
    return [(a, b) for a in range(count) for b in range(a, count)]


def tree_weights(gram, count):
    weights = [[(r, None)] for r in range(count)]
    while count > 1:
        half = count // 2
        low, high = [], []
        for i in range(half):
            aa, bb, ab = gram[2 * i, 2 * i], gram[2 * i + 1, 2 * i + 1], gram[2 * i, 2 * i + 1]
            bound = jnp.sqrt(aa) * jnp.sqrt(bb)
            ab = jnp.clip(ab, -bound, bound)
            low.append(1.0 - ab / (2.0 * (aa + epsilon)))
            high.append(1.0 - ab / (2.0 * (bb + epsilon)))
        merged = {}
        for i, j in pair_list(half):
            cross = gram[2 * i, 2 * j + 1]
            back = gram[2 * i + 1, 2 * j] if i != j else cross
            value = (
                low[i] * (low[j] * gram[2 * i, 2 * j] + high[j] * cross)
                + high[i] * (low[j] * back + high[j] * gram[2 * i + 1, 2 * j + 1])
            )
            merged[i, j] = jnp.maximum(value, 0.0) if i == j else value
        weights = [
            [(r, low[i] if w is None else w * low[i]) for r, w in weights[2 * i]]
            + [(r, high[i] if w is None else w * high[i]) for r, w in weights[2 * i + 1]]
            for i in range(half)
        ]
        gram, count = merged, half
    return [w for _, w in sorted(weights[0], key=lambda item: item[0])]


def kernel(
    R, Z, x_ref, y_ref, out_ref, fw,
    xg, yg, grads, part, first, second,
    esend, zrecv, xsend, xrecv, rsend, lsend, ysend, yrecv, psend, fsend, lsem,
    asend, arecv, bsend, brecv,
):
    me = lax.axis_index("dp")
    z = lax.axis_index("tensor")
    chips = R // 2
    last = chips - 1
    chip, core = me // 2, me % 2
    sibling = chip * 2 + 1 - core
    rows = x_ref.shape[0] // CHUNKS
    width = xg.shape[2]
    columns = yg.shape[2]

    def across(c, way):
        return (c // 2) * 2 + 1 - c % 2 if way == 0 else (1 - c // 2) * 2 + c % 2

    side, above = across(chip, 0), across(chip, 1)
    opposite = across(side, 1)
    order = (chip, side, above, opposite)
    via = jnp.where(core == 0, side, above)
    other = jnp.where(core == 0, above, side)

    barrier = pltpu.get_barrier_semaphore()
    for j in range(1, Z):
        pl.semaphore_signal(barrier, inc=1, device_id=(me, (z + j) % Z), device_id_type=MESH)
    for j in range(1, R):
        pl.semaphore_signal(barrier, inc=1, device_id=((me + j) % R, z), device_id_type=MESH)
    pl.semaphore_wait(barrier, Z + R - 2)

    def remote(src, dst, send, recv, device):
        return pltpu.make_async_remote_copy(
            src_ref=src, dst_ref=dst, send_sem=send, recv_sem=recv,
            device_id=device, device_id_type=MESH,
        )

    def go(copy, start):
        if start:
            copy.start()
        else:
            copy.wait_send()

    def span(i):
        return pl.ds(pl.multiple_of(i * rows, rows), rows)

    def half(ref, h):
        return ref.at[:, pl.ds(h * width, width)]

    def held(s, i):
        return fw.at[s, span(i)]

    def to_owner(src, r, i, h, send, dest):
        return remote(half(src, h), xg.at[r, span(i)], send, xrecv.at[r, i], (dest, z))

    def express(src, s, i, start):
        @pl.when((chip == last) & (z < Z - 1))
        def _():
            go(remote(src, held(s, i), esend.at[s, i], zrecv.at[s, i], (me, z + 1)), start)

        @pl.when((chip == 0) & (z > 0))
        def _():
            go(remote(src, held(s, i), esend.at[s, i], zrecv.at[s, i], (me, z - 1)), start)

    def own_slab(i, start):
        src = x_ref.at[span(i)]
        express(src, z, i, start)

        @pl.when(z == chip)
        def _():
            for h in range(2):
                @pl.when(h == core)
                def _():
                    if start:
                        pltpu.make_async_copy(
                            half(src, h), xg.at[me, span(i)], xrecv.at[me, i]
                        ).start()

                @pl.when(h != core)
                def _():
                    go(to_owner(src, me, i, h, xsend.at[z, i, h], sibling), start)

        @pl.when((z == side) | (z == above))
        def _():
            for h in range(2):
                go(to_owner(src, me, i, h, xsend.at[z, i, h], 2 * z + h), start)

        @pl.when(z == opposite)
        def _():
            go(
                remote(src, held(z, i), xsend.at[z, i, 0], zrecv.at[z, i], (2 * via + core, z)),
                start,
            )

    def relay(i, start):
        @pl.when(z == other)
        def _():
            r = 2 * via + core
            if start:
                remote(held(z, i), held(z, i), rsend.at[i, 0], zrecv.at[z, i], (r, z)).wait_recv()
            for h in range(2):
                go(to_owner(held(z, i), r, i, h, rsend.at[i, h], 2 * z + h), start)

    def ways(o):
        return (
            (z >= chip) & (z < Z - 1) & (o != last),
            (z <= chip) & (z > 0) & (o != 0),
        )

    def x_arrived(r, i):
        pltpu.make_async_copy(xg.at[r, span(i)], xg.at[r, span(i)], xrecv.at[r, i]).wait()

    def line(o, i, start):
        right, left = ways(o)
        for k in range(2):
            r = 2 * o + k
            if start:
                @pl.when(right | left)
                def _():
                    x_arrived(r, i)
            for way, there in ((0, right), (1, left)):
                @pl.when(there)
                def _():
                    go(
                        remote(
                            xg.at[r, span(i)], xg.at[r, span(i)], lsend.at[way, r, i],
                            xrecv.at[r, i], (me, z + 1 - 2 * way),
                        ),
                        start,
                    )

    def express_on(t, i, start):
        for s, there in (
            (z - t, (chip == last) & (z - t >= 0)),
            (z + t, (chip == 0) & (z + t < Z)),
        ):
            @pl.when(there)
            def _():
                if start:
                    remote(held(s, i), held(s, i), esend.at[s, i], zrecv.at[s, i], (me, 0)).wait_recv()
                express(held(s, i), s, i, start)
                for h in range(2):
                    go(to_owner(held(s, i), me, i, h, xsend.at[s, i, h], 2 * s + h), start)

    def y_arrived(r):
        pltpu.make_async_copy(yg.at[r], yg.at[r], yrecv.at[r]).wait()

    def y_direct(n, c):
        return remote(y_ref, yg.at[me], ysend.at[n], yrecv.at[me], (2 * c + core, z))

    def y_sibling():
        return remote(y_ref, yg.at[me], ysend.at[2], yrecv.at[me], (sibling, z))

    def y_local():
        return pltpu.make_async_copy(y_ref, yg.at[me], lsem)

    def y_relay():
        r = 2 * via + core
        return remote(yg.at[r], yg.at[r], psend, yrecv.at[r], (2 * other + core, z))

    def y_share(n):
        r = 2 * order[n] + core
        return remote(yg.at[r], yg.at[r], fsend.at[n - 1], yrecv.at[r], (sibling, z))

    tile = 256
    units = CHUNKS // FOLD

    def product(o, u):
        right, left = ways(o)
        for k in range(2):
            r = 2 * o + k

            @pl.when(jnp.logical_not(right | left))
            def _():
                for f in range(FOLD):
                    x_arrived(r, u * FOLD + f)

            at_k = pl.ds(pl.multiple_of(u * FOLD * rows, FOLD * rows), FOLD * rows)

            @pl.loop(0, columns // tile)
            def _(q):
                at = pl.ds(pl.multiple_of(q * tile, tile), tile)
                value = lax.dot_general(
                    xg[r, at_k, :], yg[r, at_k, at], (((0,), (0,)), ((), ())),
                    preferred_element_type=jnp.float32,
                )

                @pl.when(u == 0)
                def _():
                    grads[r, :, at] = value

                @pl.when(u > 0)
                def _():
                    grads[r, :, at] += value

    @pl.loop(0, CHUNKS)
    def _(i):
        own_slab(i, True)

    @pl.loop(0, CHUNKS)
    def _(i):
        line(order[0], i, True)
        relay(i, True)
        express_on(1, i, True)

        @pl.when(i == CHUNKS // 4)
        def _():
            y_sibling().start()
            y_direct(0, via).start()
            y_direct(1, other).start()
            y_local().start()

    y_local().wait()
    y_arrived(sibling)

    @pl.loop(0, CHUNKS)
    def _(i):
        line(order[1], i, True)
        express_on(2, i, True)

        @pl.when(i >= CHUNKS - units)
        def _():
            product(order[0], i - (CHUNKS - units))

    y_arrived(2 * via + core)
    y_relay().start()
    y_arrived(2 * other + core)
    for n in (1, 2):
        y_share(n).start()

    @pl.loop(0, CHUNKS)
    def _(i):
        line(order[2], i, True)
        express_on(3, i, True)

        @pl.when(i == CHUNKS - units)
        def _():
            y_arrived(2 * side + 1 - core)
            y_arrived(2 * above + 1 - core)

        @pl.when(i >= CHUNKS - units)
        def _():
            product(order[1], i - (CHUNKS - units))

    y_arrived(2 * opposite + core)
    y_share(3).start()

    @pl.loop(0, CHUNKS)
    def _(i):
        line(order[3], i, True)

    @pl.loop(0, units)
    def _(u):
        product(order[2], u)

    y_arrived(2 * opposite + 1 - core)

    @pl.loop(0, units)
    def _(u):
        product(order[3], u)

    pairs = pair_list(R)

    def accumulate(b, sums):
        at = pl.ds(pl.multiple_of(b * 8, 8), 8)
        sums = list(sums)
        for q in range(columns // 128):
            blocks = [grads[r, at, pl.ds(q * 128, 128)] for r in range(R)]
            for n, (a, c) in enumerate(pairs):
                sums[n] = sums[n] + blocks[a] * blocks[c]
        return tuple(sums)

    sums = lax.fori_loop(
        0, width // 8, accumulate, tuple(jnp.zeros((8, 128), jnp.float32) for _ in pairs)
    )
    part[0] = jnp.zeros(part.shape[1:], jnp.float32)
    for n in range(len(pairs)):
        part[0, pl.ds(n, 1), :] = jnp.sum(sums[n], axis=0, keepdims=True)

    def around_z(j):
        return remote(part.at[0], first.at[j - 1], asend.at[j - 1], arecv.at[j - 1], (me, (z + j) % Z))

    def around_plane(j):
        return remote(
            part.at[1], second.at[j - 1], bsend.at[j - 1], brecv.at[j - 1], ((me + j) % R, z)
        )

    for j in range(1, Z):
        around_z(j).start()
    for j in range(1, Z):
        around_z(j).wait_recv()
    part[1] = part[0] + sum(first[j - 1] for j in range(1, Z))
    for j in range(1, R):
        around_plane(j).start()
    for j in range(1, R):
        around_plane(j).wait_recv()
    totals = part[1] + sum(second[j - 1] for j in range(1, R))
    totals = jnp.sum(totals, axis=1, keepdims=True)
    gram = {pair: totals[n:n + 1, :] for n, pair in enumerate(pairs)}
    weights = tree_weights(gram, R)

    band = 16

    @pl.loop(0, width // band)
    def _(b):
        at = pl.ds(pl.multiple_of(b * band, band), band)
        total = weights[0] * grads[0, at, :]
        for r in range(1, R):
            total = total + weights[r] * grads[r, at, :]
        out_ref[at, :] = total

    @pl.loop(0, CHUNKS)
    def _(i):
        own_slab(i, False)
        relay(i, False)
        for n in range(4):
            line(order[n], i, False)
        for t in range(1, 4):
            express_on(t, i, False)

    y_sibling().wait_send()
    y_direct(0, via).wait_send()
    y_direct(1, other).wait_send()
    y_relay().wait_send()
    for n in (1, 2, 3):
        y_share(n).wait_send()
    for j in range(1, Z):
        around_z(j).wait_send()
    for j in range(1, R):
        around_plane(j).wait_send()


def by_tiles(R, Z, activations, out_grads):
    tokens, slab = activations.shape
    columns = out_grads.shape[1]
    width = slab * Z // R
    kept = -(-len(pair_list(R)) // 8) * 8
    dma = pltpu.SemaphoreType.DMA
    return pl.pallas_call(
        functools.partial(kernel, R, Z),
        out_shape=(
            jax.ShapeDtypeStruct((width, columns), jnp.float32),
            jax.ShapeDtypeStruct((Z, tokens, slab), jnp.bfloat16),
        ),
        in_specs=[pl.BlockSpec(memory_space=pl.ANY)] * 2,
        out_specs=(
            pl.BlockSpec(memory_space=pltpu.VMEM),
            pl.BlockSpec(memory_space=pl.ANY),
        ),
        scratch_shapes=[
            pltpu.VMEM((R, tokens, width), jnp.bfloat16),
            pltpu.VMEM((R, tokens, columns), jnp.bfloat16),
            pltpu.VMEM((R, width, columns), jnp.float32),
            pltpu.VMEM((2, kept, 128), jnp.float32),
            pltpu.VMEM((Z - 1, kept, 128), jnp.float32),
            pltpu.VMEM((R - 1, kept, 128), jnp.float32),
            dma((Z, CHUNKS)),
            dma((Z, CHUNKS)),
            dma((Z, CHUNKS, 2)),
            dma((R, CHUNKS)),
            dma((CHUNKS, 2)),
            dma((2, R, CHUNKS)),
            dma((3,)),
            dma((R,)),
            dma,
            dma((3,)),
            dma,
            dma((Z - 1,)),
            dma((Z - 1,)),
            dma((R - 1,)),
            dma((R - 1,)),
        ],
        compiler_params=pltpu.CompilerParams(
            collective_id=0, has_side_effects=True, vmem_limit_bytes=60 * 1024 * 1024
        ),
        cost_estimate=pl.CostEstimate(
            flops=2 * R * tokens * width * columns,
            bytes_accessed=2 * R * tokens * (width + columns),
            transcendentals=0,
        ),
    )(activations, out_grads)[0]


def solution(mesh):
    R, Z = mesh.shape["dp"], mesh.shape["tensor"]

    def on_device(activations, out_grads):
        tokens, slab = activations.shape
        columns = out_grads.shape[1]
        width = slab * Z // R
        fits = (
            R == 8 and Z == 4 and width % 128 == 0 and columns % 256 == 0
            and tokens % (CHUNKS * 16) == 0
            and R * (2 * tokens * (width + columns) + 4 * width * columns) < 50 * 2**20
        )
        if fits:
            return by_tiles(R, Z, activations, out_grads)
        return by_halving(activations, out_grads)

    return jax.shard_map(
        on_device,
        mesh=mesh,
        in_specs=(P("dp", "tensor"), P("dp", "tensor")),
        out_specs=P("dp", "tensor"),
        check_vma=False,
    )
```

```python
import functools
import jax
import jax.numpy as jnp
from jax import lax
from jax.experimental import pallas as pl
from jax.experimental.pallas import tpu as pltpu
from jax.sharding import PartitionSpec as P

epsilon = 1e-06
MESH = pl.DeviceIdType.MESH
CHUNKS = 8
FOLD = 4


def swapped(x, axis, apart):
    return lax.ppermute(x, axis, [(i, i ^ 1 << apart) for i in range(lax.axis_size(axis))])


def group_totals(partials, section):
    for bit_number in range(section + 1):
        partials = partials + swapped(partials, "dp", bit_number)
    return lax.psum(partials, "tensor")


def adasum_pair(mine, other, section, replica):
    upper_side = jnp.right_shift(replica, section) % 2 == 1
    mine_norm = jnp.sum(mine * mine)
    other_norm = jnp.sum(other * other)
    lower_norm = jnp.where(upper_side, other_norm, mine_norm)
    upper_norm = jnp.where(upper_side, mine_norm, other_norm)
    partials = jnp.stack([jnp.sum(mine * other), lower_norm, upper_norm])
    totals = group_totals(partials, section)
    lower_coef = 1.0 - totals[0] / (2.0 * (totals[1] + epsilon))
    upper_coef = 1.0 - totals[0] / (2.0 * (totals[2] + epsilon))
    mine_coef = jnp.where(upper_side, upper_coef, lower_coef)
    other_coef = jnp.where(upper_side, lower_coef, upper_coef)
    return mine_coef * mine + other_coef * other


def by_halving(activations, out_grads):
    replicas = lax.axis_size("dp")
    section_count = replicas.bit_length() - 1
    replica = lax.axis_index("dp")
    columns = out_grads.shape[1]
    slab_rows = activations.shape[1]
    block_rows = slab_rows * lax.axis_size("tensor") // replicas
    full_grad = jnp.einsum(
        "tk,tf->kf",
        lax.all_gather(activations, "tensor", axis=1, tiled=True),
        out_grads,
        preferred_element_type=jnp.float32,
    )
    holding = full_grad.reshape(replicas, block_rows, columns)
    for section in range(section_count):
        section_bit = jnp.right_shift(replica, section) % 2
        paired = holding.reshape(-1, 2, block_rows, columns)
        keeping = lax.dynamic_index_in_dim(paired, section_bit, axis=1, keepdims=False)
        sending = lax.dynamic_index_in_dim(paired, 1 - section_bit, axis=1, keepdims=False)
        received = swapped(sending, "dp", section)
        holding = adasum_pair(keeping, received, section, replica)
    return holding.reshape(block_rows, columns)


def pair_list(count):
    return [(a, b) for a in range(count) for b in range(a, count)]


def tree_weights(gram, count):
    weights = [[(r, None)] for r in range(count)]
    while count > 1:
        half = count // 2
        low, high = [], []
        for i in range(half):
            aa, bb, ab = gram[2 * i, 2 * i], gram[2 * i + 1, 2 * i + 1], gram[2 * i, 2 * i + 1]
            bound = jnp.sqrt(aa) * jnp.sqrt(bb)
            ab = jnp.clip(ab, -bound, bound)
            low.append(1.0 - ab / (2.0 * (aa + epsilon)))
            high.append(1.0 - ab / (2.0 * (bb + epsilon)))
        merged = {}
        for i, j in pair_list(half):
            cross = gram[2 * i, 2 * j + 1]
            back = gram[2 * i + 1, 2 * j] if i != j else cross
            value = (
                low[i] * (low[j] * gram[2 * i, 2 * j] + high[j] * cross)
                + high[i] * (low[j] * back + high[j] * gram[2 * i + 1, 2 * j + 1])
            )
            merged[i, j] = jnp.maximum(value, 0.0) if i == j else value
        weights = [
            [(r, low[i] if w is None else w * low[i]) for r, w in weights[2 * i]]
            + [(r, high[i] if w is None else w * high[i]) for r, w in weights[2 * i + 1]]
            for i in range(half)
        ]
        gram, count = merged, half
    return [w for _, w in sorted(weights[0], key=lambda item: item[0])]


def kernel(
    R, Z, x_ref, y_ref, out_ref, fw,
    xg, yg, grads, part, first, second,
    esend, zrecv, xsend, xrecv, rsend, lsend, ysend, yrecv, psend, fsend, lsem,
    asend, arecv, bsend, brecv,
):
    me = lax.axis_index("dp")
    z = lax.axis_index("tensor")
    chips = R // 2
    last = chips - 1
    chip, core = me // 2, me % 2
    sibling = chip * 2 + 1 - core
    width = xg.shape[1]
    rows = width // CHUNKS
    columns = yg.shape[2]

    def across(c, way):
        return (c // 2) * 2 + 1 - c % 2 if way == 0 else (1 - c // 2) * 2 + c % 2

    side, above = across(chip, 0), across(chip, 1)
    opposite = across(side, 1)
    order = (chip, side, above, opposite)
    via = jnp.where(core == 0, side, above)
    other = jnp.where(core == 0, above, side)

    barrier = pltpu.get_barrier_semaphore()
    for j in range(1, Z):
        pl.semaphore_signal(barrier, inc=1, device_id=(me, (z + j) % Z), device_id_type=MESH)
    for j in range(1, R):
        pl.semaphore_signal(barrier, inc=1, device_id=((me + j) % R, z), device_id_type=MESH)
    pl.semaphore_wait(barrier, Z + R - 2)

    def remote(src, dst, send, recv, device):
        return pltpu.make_async_remote_copy(
            src_ref=src, dst_ref=dst, send_sem=send, recv_sem=recv,
            device_id=device, device_id_type=MESH,
        )

    def go(copy, start):
        if start:
            copy.start()
        else:
            copy.wait_send()

    def span(i):
        return pl.ds(pl.multiple_of(i * rows, rows), rows)

    def held(s, i):
        return fw.at[s, :, span(i)]

    def to_owner(src, r, i, h, send, dest):
        return remote(src.at[h], xg.at[r, span(i)], send, xrecv.at[r, i], (dest, z))

    def express(src, s, i, start):
        @pl.when((chip == last) & (z < Z - 1))
        def _():
            go(remote(src, held(s, i), esend.at[s, i], zrecv.at[s, i], (me, z + 1)), start)

        @pl.when((chip == 0) & (z > 0))
        def _():
            go(remote(src, held(s, i), esend.at[s, i], zrecv.at[s, i], (me, z - 1)), start)

    def own_slab(i, start):
        src = x_ref.at[:, span(i)]
        express(src, z, i, start)

        @pl.when(z == chip)
        def _():
            for h in range(2):
                @pl.when(h == core)
                def _():
                    if start:
                        pltpu.make_async_copy(
                            src.at[h], xg.at[me, span(i)], xrecv.at[me, i]
                        ).start()

                @pl.when(h != core)
                def _():
                    go(to_owner(src, me, i, h, xsend.at[z, i, h], sibling), start)

        @pl.when((z == side) | (z == above))
        def _():
            for h in range(2):
                go(to_owner(src, me, i, h, xsend.at[z, i, h], 2 * z + h), start)

        @pl.when(z == opposite)
        def _():
            go(
                remote(src, held(z, i), xsend.at[z, i, 0], zrecv.at[z, i], (2 * via + core, z)),
                start,
            )

    def relay(i, start):
        @pl.when(z == other)
        def _():
            r = 2 * via + core
            if start:
                remote(held(z, i), held(z, i), rsend.at[i, 0], zrecv.at[z, i], (r, z)).wait_recv()
            for h in range(2):
                go(to_owner(held(z, i), r, i, h, rsend.at[i, h], 2 * z + h), start)

    def ways(o):
        return (
            (z >= chip) & (z < Z - 1) & (o != last),
            (z <= chip) & (z > 0) & (o != 0),
        )

    def x_arrived(r, i):
        pltpu.make_async_copy(xg.at[r, span(i)], xg.at[r, span(i)], xrecv.at[r, i]).wait()

    def line(o, i, start):
        right, left = ways(o)
        for k in range(2):
            r = 2 * o + k
            if start:
                @pl.when(right | left)
                def _():
                    x_arrived(r, i)
            for way, there in ((0, right), (1, left)):
                @pl.when(there)
                def _():
                    go(
                        remote(
                            xg.at[r, span(i)], xg.at[r, span(i)], lsend.at[way, r, i],
                            xrecv.at[r, i], (me, z + 1 - 2 * way),
                        ),
                        start,
                    )

    def express_on(t, i, start):
        for s, there in (
            (z - t, (chip == last) & (z - t >= 0)),
            (z + t, (chip == 0) & (z + t < Z)),
        ):
            @pl.when(there)
            def _():
                if start:
                    remote(held(s, i), held(s, i), esend.at[s, i], zrecv.at[s, i], (me, 0)).wait_recv()
                express(held(s, i), s, i, start)
                for h in range(2):
                    go(to_owner(held(s, i), me, i, h, xsend.at[s, i, h], 2 * s + h), start)

    def y_arrived(r):
        pltpu.make_async_copy(yg.at[r], yg.at[r], yrecv.at[r]).wait()

    def y_direct(n, c):
        return remote(y_ref, yg.at[me], ysend.at[n], yrecv.at[me], (2 * c + core, z))

    def y_sibling():
        return remote(y_ref, yg.at[me], ysend.at[2], yrecv.at[me], (sibling, z))

    def y_local():
        return pltpu.make_async_copy(y_ref, yg.at[me], lsem)

    def y_relay():
        r = 2 * via + core
        return remote(yg.at[r], yg.at[r], psend, yrecv.at[r], (2 * other + core, z))

    def y_share(n):
        r = 2 * order[n] + core
        return remote(yg.at[r], yg.at[r], fsend.at[n - 1], yrecv.at[r], (sibling, z))

    tile = 256
    units = CHUNKS // FOLD

    def product(o, u):
        right, left = ways(o)
        for k in range(2):
            r = 2 * o + k

            @pl.when(jnp.logical_not(right | left))
            def _():
                for f in range(FOLD):
                    x_arrived(r, u * FOLD + f)

            block = pl.ds(pl.multiple_of(u * FOLD * rows, FOLD * rows), FOLD * rows)

            @pl.loop(0, columns // tile)
            def _(q):
                at = pl.ds(pl.multiple_of(q * tile, tile), tile)
                grads[r, block, at] = jnp.dot(
                    xg[r, block, :], yg[r, :, at], preferred_element_type=jnp.float32
                )

    @pl.loop(0, CHUNKS)
    def _(i):
        own_slab(i, True)

    @pl.loop(0, CHUNKS)
    def _(i):
        line(order[0], i, True)
        relay(i, True)
        express_on(1, i, True)

        @pl.when(i == CHUNKS // 4)
        def _():
            y_sibling().start()
            y_direct(0, via).start()
            y_direct(1, other).start()
            y_local().start()

    y_local().wait()
    y_arrived(sibling)

    @pl.loop(0, CHUNKS)
    def _(i):
        line(order[1], i, True)
        express_on(2, i, True)

        @pl.when(i >= CHUNKS - units)
        def _():
            product(order[0], i - (CHUNKS - units))

    y_arrived(2 * via + core)
    y_relay().start()
    y_arrived(2 * other + core)
    for n in (1, 2):
        y_share(n).start()

    @pl.loop(0, CHUNKS)
    def _(i):
        line(order[2], i, True)
        express_on(3, i, True)

        @pl.when(i == CHUNKS - units)
        def _():
            y_arrived(2 * side + 1 - core)
            y_arrived(2 * above + 1 - core)

        @pl.when(i >= CHUNKS - units)
        def _():
            product(order[1], i - (CHUNKS - units))

    y_arrived(2 * opposite + core)
    y_share(3).start()

    @pl.loop(0, CHUNKS)
    def _(i):
        line(order[3], i, True)

    @pl.loop(0, units)
    def _(u):
        product(order[2], u)

    y_arrived(2 * opposite + 1 - core)

    @pl.loop(0, units)
    def _(u):
        product(order[3], u)

    pairs = pair_list(R)

    def accumulate(b, sums):
        at = pl.ds(pl.multiple_of(b * 8, 8), 8)
        sums = list(sums)
        for q in range(columns // 128):
            blocks = [grads[r, at, pl.ds(q * 128, 128)] for r in range(R)]
            for n, (a, c) in enumerate(pairs):
                sums[n] = sums[n] + blocks[a] * blocks[c]
        return tuple(sums)

    sums = lax.fori_loop(
        0, width // 8, accumulate, tuple(jnp.zeros((8, 128), jnp.float32) for _ in pairs)
    )
    part[0] = jnp.zeros(part.shape[1:], jnp.float32)
    for n in range(len(pairs)):
        part[0, pl.ds(n, 1), :] = jnp.sum(sums[n], axis=0, keepdims=True)

    def around_z(j):
        return remote(part.at[0], first.at[j - 1], asend.at[j - 1], arecv.at[j - 1], (me, (z + j) % Z))

    def around_plane(j):
        return remote(
            part.at[1], second.at[j - 1], bsend.at[j - 1], brecv.at[j - 1], ((me + j) % R, z)
        )

    for j in range(1, Z):
        around_z(j).start()
    for j in range(1, Z):
        around_z(j).wait_recv()
    part[1] = part[0] + sum(first[j - 1] for j in range(1, Z))
    for j in range(1, R):
        around_plane(j).start()
    for j in range(1, R):
        around_plane(j).wait_recv()
    totals = part[1] + sum(second[j - 1] for j in range(1, R))
    totals = jnp.sum(totals, axis=1, keepdims=True)
    gram = {pair: totals[n:n + 1, :] for n, pair in enumerate(pairs)}
    weights = tree_weights(gram, R)

    band = 16

    @pl.loop(0, width // band)
    def _(b):
        at = pl.ds(pl.multiple_of(b * band, band), band)
        total = weights[0] * grads[0, at, :]
        for r in range(1, R):
            total = total + weights[r] * grads[r, at, :]
        out_ref[at, :] = total

    @pl.loop(0, CHUNKS)
    def _(i):
        own_slab(i, False)
        relay(i, False)
        for n in range(4):
            line(order[n], i, False)
        for t in range(1, 4):
            express_on(t, i, False)

    y_sibling().wait_send()
    y_direct(0, via).wait_send()
    y_direct(1, other).wait_send()
    y_relay().wait_send()
    for n in (1, 2, 3):
        y_share(n).wait_send()
    for j in range(1, Z):
        around_z(j).wait_send()
    for j in range(1, R):
        around_plane(j).wait_send()


def by_tiles(R, Z, activations, out_grads):
    tokens, slab = activations.shape
    columns = out_grads.shape[1]
    width = slab * Z // R
    kept = -(-len(pair_list(R)) // 8) * 8
    dma = pltpu.SemaphoreType.DMA
    return pl.pallas_call(
        functools.partial(kernel, R, Z),
        out_shape=(
            jax.ShapeDtypeStruct((width, columns), jnp.float32),
            jax.ShapeDtypeStruct((Z, 2, width, tokens), jnp.bfloat16),
        ),
        in_specs=[pl.BlockSpec(memory_space=pl.ANY)] * 2,
        out_specs=(
            pl.BlockSpec(memory_space=pltpu.VMEM),
            pl.BlockSpec(memory_space=pl.ANY),
        ),
        scratch_shapes=[
            pltpu.VMEM((R, width, tokens), jnp.bfloat16),
            pltpu.VMEM((R, tokens, columns), jnp.bfloat16),
            pltpu.VMEM((R, width, columns), jnp.float32),
            pltpu.VMEM((2, kept, 128), jnp.float32),
            pltpu.VMEM((Z - 1, kept, 128), jnp.float32),
            pltpu.VMEM((R - 1, kept, 128), jnp.float32),
            dma((Z, CHUNKS)),
            dma((Z, CHUNKS)),
            dma((Z, CHUNKS, 2)),
            dma((R, CHUNKS)),
            dma((CHUNKS, 2)),
            dma((2, R, CHUNKS)),
            dma((3,)),
            dma((R,)),
            dma,
            dma((3,)),
            dma,
            dma((Z - 1,)),
            dma((Z - 1,)),
            dma((R - 1,)),
            dma((R - 1,)),
        ],
        compiler_params=pltpu.CompilerParams(
            collective_id=0, has_side_effects=True, vmem_limit_bytes=60 * 1024 * 1024
        ),
        cost_estimate=pl.CostEstimate(
            flops=2 * R * tokens * width * columns,
            bytes_accessed=2 * R * tokens * (width + columns),
            transcendentals=0,
        ),
    )(activations.T.reshape(2, width, tokens), out_grads)[0]


def solution(mesh):
    R, Z = mesh.shape["dp"], mesh.shape["tensor"]

    def on_device(activations, out_grads):
        tokens, slab = activations.shape
        columns = out_grads.shape[1]
        width = slab * Z // R
        fits = (
            R == 8 and Z == 4 and width % 128 == 0 and columns % 256 == 0
            and tokens % 128 == 0 and width % (CHUNKS * 16) == 0
            and R * (2 * tokens * (width + columns) + 4 * width * columns) < 50 * 2**20
        )
        if fits:
            return by_tiles(R, Z, activations, out_grads)
        return by_halving(activations, out_grads)

    return jax.shard_map(
        on_device,
        mesh=mesh,
        in_specs=(P("dp", "tensor"), P("dp", "tensor")),
        out_specs=P("dp", "tensor"),
        check_vma=False,
    )
```

```python
import functools
import jax
import jax.numpy as jnp
from jax import lax
from jax.experimental import pallas as pl
from jax.experimental.pallas import tpu as pltpu
from jax.sharding import PartitionSpec as P

epsilon = 1e-06
MESH = pl.DeviceIdType.MESH
CHUNKS = 20
FOLD = 10


def swapped(x, axis, apart):
    return lax.ppermute(x, axis, [(i, i ^ 1 << apart) for i in range(lax.axis_size(axis))])


def group_totals(partials, section):
    for bit_number in range(section + 1):
        partials = partials + swapped(partials, "dp", bit_number)
    return lax.psum(partials, "tensor")


def adasum_pair(mine, other, section, replica):
    upper_side = jnp.right_shift(replica, section) % 2 == 1
    mine_norm = jnp.sum(mine * mine)
    other_norm = jnp.sum(other * other)
    lower_norm = jnp.where(upper_side, other_norm, mine_norm)
    upper_norm = jnp.where(upper_side, mine_norm, other_norm)
    partials = jnp.stack([jnp.sum(mine * other), lower_norm, upper_norm])
    totals = group_totals(partials, section)
    lower_coef = 1.0 - totals[0] / (2.0 * (totals[1] + epsilon))
    upper_coef = 1.0 - totals[0] / (2.0 * (totals[2] + epsilon))
    mine_coef = jnp.where(upper_side, upper_coef, lower_coef)
    other_coef = jnp.where(upper_side, lower_coef, upper_coef)
    return mine_coef * mine + other_coef * other


def by_halving(activations, out_grads):
    replicas = lax.axis_size("dp")
    section_count = replicas.bit_length() - 1
    replica = lax.axis_index("dp")
    columns = out_grads.shape[1]
    slab_rows = activations.shape[1]
    block_rows = slab_rows * lax.axis_size("tensor") // replicas
    full_grad = jnp.einsum(
        "tk,tf->kf",
        lax.all_gather(activations, "tensor", axis=1, tiled=True),
        out_grads,
        preferred_element_type=jnp.float32,
    )
    holding = full_grad.reshape(replicas, block_rows, columns)
    for section in range(section_count):
        section_bit = jnp.right_shift(replica, section) % 2
        paired = holding.reshape(-1, 2, block_rows, columns)
        keeping = lax.dynamic_index_in_dim(paired, section_bit, axis=1, keepdims=False)
        sending = lax.dynamic_index_in_dim(paired, 1 - section_bit, axis=1, keepdims=False)
        received = swapped(sending, "dp", section)
        holding = adasum_pair(keeping, received, section, replica)
    return holding.reshape(block_rows, columns)


def pair_list(count):
    return [(a, b) for a in range(count) for b in range(a, count)]


def tree_weights(gram, count):
    weights = [[(r, None)] for r in range(count)]
    while count > 1:
        half = count // 2
        low, high = [], []
        for i in range(half):
            aa, bb, ab = gram[2 * i, 2 * i], gram[2 * i + 1, 2 * i + 1], gram[2 * i, 2 * i + 1]
            bound = jnp.sqrt(aa) * jnp.sqrt(bb)
            ab = jnp.clip(ab, -bound, bound)
            low.append(1.0 - ab / (2.0 * (aa + epsilon)))
            high.append(1.0 - ab / (2.0 * (bb + epsilon)))
        merged = {}
        for i, j in pair_list(half):
            cross = gram[2 * i, 2 * j + 1]
            back = gram[2 * i + 1, 2 * j] if i != j else cross
            value = (
                low[i] * (low[j] * gram[2 * i, 2 * j] + high[j] * cross)
                + high[i] * (low[j] * back + high[j] * gram[2 * i + 1, 2 * j + 1])
            )
            merged[i, j] = jnp.maximum(value, 0.0) if i == j else value
        weights = [
            [(r, low[i] if w is None else w * low[i]) for r, w in weights[2 * i]]
            + [(r, high[i] if w is None else w * high[i]) for r, w in weights[2 * i + 1]]
            for i in range(half)
        ]
        gram, count = merged, half
    return [w for _, w in sorted(weights[0], key=lambda item: item[0])]


def kernel(
    R, Z, x_ref, y_ref, out_ref, fw,
    xg, yg, grads, part, first, second,
    esend, zrecv, xsend, xrecv, rsend, lsend, ysend, yrecv, psend, fsend, lsem,
    asend, arecv, bsend, brecv,
):
    me = lax.axis_index("dp")
    z = lax.axis_index("tensor")
    chips = R // 2
    last = chips - 1
    chip, core = me // 2, me % 2
    sibling = chip * 2 + 1 - core
    width = xg.shape[1]
    rows = width // CHUNKS
    columns = yg.shape[2]

    def across(c, way):
        return (c // 2) * 2 + 1 - c % 2 if way == 0 else (1 - c // 2) * 2 + c % 2

    side, above = across(chip, 0), across(chip, 1)
    opposite = across(side, 1)
    order = (chip, side, above, opposite)
    via = jnp.where(core == 0, side, above)
    other = jnp.where(core == 0, above, side)

    barrier = pltpu.get_barrier_semaphore()
    for j in range(1, Z):
        pl.semaphore_signal(barrier, inc=1, device_id=(me, (z + j) % Z), device_id_type=MESH)
    for j in range(1, R):
        pl.semaphore_signal(barrier, inc=1, device_id=((me + j) % R, z), device_id_type=MESH)
    pl.semaphore_wait(barrier, Z + R - 2)

    def remote(src, dst, send, recv, device):
        return pltpu.make_async_remote_copy(
            src_ref=src, dst_ref=dst, send_sem=send, recv_sem=recv,
            device_id=device, device_id_type=MESH,
        )

    def go(copy, start):
        if start:
            copy.start()
        else:
            copy.wait_send()

    def span(i):
        return pl.ds(pl.multiple_of(i * rows, rows), rows)

    def held(s, i):
        return fw.at[s, :, span(i)]

    def to_owner(src, r, i, h, send, dest):
        return remote(src.at[h], xg.at[r, span(i)], send, xrecv.at[r, i], (dest, z))

    def express(src, s, i, start):
        @pl.when((chip == last) & (z < Z - 1))
        def _():
            go(remote(src, held(s, i), esend.at[s, i], zrecv.at[s, i], (me, z + 1)), start)

        @pl.when((chip == 0) & (z > 0))
        def _():
            go(remote(src, held(s, i), esend.at[s, i], zrecv.at[s, i], (me, z - 1)), start)

    def own_slab(i, start):
        src = x_ref.at[:, span(i)]
        express(src, z, i, start)

        @pl.when(z == chip)
        def _():
            for h in range(2):
                @pl.when(h == core)
                def _():
                    if start:
                        pltpu.make_async_copy(
                            src.at[h], xg.at[me, span(i)], xrecv.at[me, i]
                        ).start()

                @pl.when(h != core)
                def _():
                    go(to_owner(src, me, i, h, xsend.at[z, i, h], sibling), start)

        @pl.when((z == side) | (z == above))
        def _():
            for h in range(2):
                go(to_owner(src, me, i, h, xsend.at[z, i, h], 2 * z + h), start)

        @pl.when(z == opposite)
        def _():
            go(
                remote(src, held(z, i), xsend.at[z, i, 0], zrecv.at[z, i], (2 * via + core, z)),
                start,
            )

    def relay(i, start):
        @pl.when(z == other)
        def _():
            r = 2 * via + core
            if start:
                remote(held(z, i), held(z, i), rsend.at[i, 0], zrecv.at[z, i], (r, z)).wait_recv()
            for h in range(2):
                go(to_owner(held(z, i), r, i, h, rsend.at[i, h], 2 * z + h), start)

    def ways(o):
        return (
            (z >= chip) & (z < Z - 1) & (o != last),
            (z <= chip) & (z > 0) & (o != 0),
        )

    def x_arrived(r, i):
        pltpu.make_async_copy(xg.at[r, span(i)], xg.at[r, span(i)], xrecv.at[r, i]).wait()

    def line(o, i, start):
        right, left = ways(o)
        for k in range(2):
            r = 2 * o + k
            if start:
                @pl.when(right | left)
                def _():
                    x_arrived(r, i)
            for way, there in ((0, right), (1, left)):
                @pl.when(there)
                def _():
                    go(
                        remote(
                            xg.at[r, span(i)], xg.at[r, span(i)], lsend.at[way, r, i],
                            xrecv.at[r, i], (me, z + 1 - 2 * way),
                        ),
                        start,
                    )

    def pace(n, i):
        @pl.when((z == chip) & (i > 0))
        def _():
            line(order[n], i - 1, False)

        if n > 0:
            @pl.when((z == chip) & (i == 0))
            def _():
                line(order[n - 1], CHUNKS - 1, False)

    def express_on(t, i, start):
        for s, there in (
            (z - t, (chip == last) & (z - t >= 0)),
            (z + t, (chip == 0) & (z + t < Z)),
        ):
            @pl.when(there)
            def _():
                if start:
                    remote(held(s, i), held(s, i), esend.at[s, i], zrecv.at[s, i], (me, 0)).wait_recv()
                express(held(s, i), s, i, start)
                for h in range(2):
                    go(to_owner(held(s, i), me, i, h, xsend.at[s, i, h], 2 * s + h), start)

    def y_arrived(r):
        pltpu.make_async_copy(yg.at[r], yg.at[r], yrecv.at[r]).wait()

    def y_direct(n, c):
        return remote(y_ref, yg.at[me], ysend.at[n], yrecv.at[me], (2 * c + core, z))

    def y_sibling():
        return remote(y_ref, yg.at[me], ysend.at[2], yrecv.at[me], (sibling, z))

    def y_local():
        return pltpu.make_async_copy(y_ref, yg.at[me], lsem)

    def y_relay():
        r = 2 * via + core
        return remote(yg.at[r], yg.at[r], psend, yrecv.at[r], (2 * other + core, z))

    def y_share(n):
        r = 2 * order[n] + core
        return remote(yg.at[r], yg.at[r], fsend.at[n - 1], yrecv.at[r], (sibling, z))

    tile = 256
    units = CHUNKS // FOLD

    def product(o, u):
        right, left = ways(o)
        for k in range(2):
            r = 2 * o + k

            @pl.when(jnp.logical_not(right | left))
            def _():
                for f in range(FOLD):
                    x_arrived(r, u * FOLD + f)

            block = pl.ds(pl.multiple_of(u * FOLD * rows, FOLD * rows), FOLD * rows)

            @pl.loop(0, columns // tile)
            def _(q):
                at = pl.ds(pl.multiple_of(q * tile, tile), tile)
                grads[r, block, at] = jnp.dot(
                    xg[r, block, :], yg[r, :, at], preferred_element_type=jnp.float32
                )

    @pl.loop(0, CHUNKS)
    def _(i):
        own_slab(i, True)
        line(order[0], i, True)
        pace(0, i)
        relay(i, True)
        express_on(1, i, True)

        @pl.when(i == CHUNKS // 2)
        def _():
            y_sibling().start()
            y_direct(0, via).start()
            y_direct(1, other).start()
            y_local().start()

    y_local().wait()
    y_arrived(sibling)

    @pl.loop(0, CHUNKS)
    def _(i):
        line(order[1], i, True)
        pace(1, i)
        express_on(2, i, True)

        @pl.when(i >= CHUNKS - units)
        def _():
            product(order[0], i - (CHUNKS - units))

    y_arrived(2 * via + core)
    y_relay().start()
    y_arrived(2 * other + core)
    for n in (1, 2):
        y_share(n).start()

    @pl.loop(0, CHUNKS)
    def _(i):
        line(order[2], i, True)
        pace(2, i)
        express_on(3, i, True)

        @pl.when(i == CHUNKS - units)
        def _():
            y_arrived(2 * side + 1 - core)
            y_arrived(2 * above + 1 - core)

        @pl.when(i >= CHUNKS - units)
        def _():
            product(order[1], i - (CHUNKS - units))

    y_arrived(2 * opposite + core)
    y_share(3).start()

    @pl.loop(0, CHUNKS)
    def _(i):
        line(order[3], i, True)
        pace(3, i)

    @pl.loop(0, units)
    def _(u):
        product(order[2], u)

    y_arrived(2 * opposite + 1 - core)

    @pl.loop(0, units)
    def _(u):
        product(order[3], u)

    pairs = pair_list(R)

    def accumulate(b, sums):
        at = pl.ds(pl.multiple_of(b * 8, 8), 8)
        sums = list(sums)
        for q in range(columns // 128):
            blocks = [grads[r, at, pl.ds(q * 128, 128)] for r in range(R)]
            for n, (a, c) in enumerate(pairs):
                sums[n] = sums[n] + blocks[a] * blocks[c]
        return tuple(sums)

    sums = lax.fori_loop(
        0, width // 8, accumulate, tuple(jnp.zeros((8, 128), jnp.float32) for _ in pairs)
    )
    part[0] = jnp.zeros(part.shape[1:], jnp.float32)
    for n in range(len(pairs)):
        part[0, pl.ds(n, 1), :] = jnp.sum(sums[n], axis=0, keepdims=True)

    def around_z(j):
        return remote(part.at[0], first.at[j - 1], asend.at[j - 1], arecv.at[j - 1], (me, (z + j) % Z))

    def around_plane(j):
        return remote(
            part.at[1], second.at[j - 1], bsend.at[j - 1], brecv.at[j - 1], ((me + j) % R, z)
        )

    for j in range(1, Z):
        around_z(j).start()
    for j in range(1, Z):
        around_z(j).wait_recv()
    part[1] = part[0] + sum(first[j - 1] for j in range(1, Z))
    for j in range(1, R):
        around_plane(j).start()
    for j in range(1, R):
        around_plane(j).wait_recv()
    totals = part[1] + sum(second[j - 1] for j in range(1, R))
    totals = jnp.sum(totals, axis=1, keepdims=True)
    gram = {pair: totals[n:n + 1, :] for n, pair in enumerate(pairs)}
    weights = tree_weights(gram, R)

    band = 16

    @pl.loop(0, width // band)
    def _(b):
        at = pl.ds(pl.multiple_of(b * band, band), band)
        total = weights[0] * grads[0, at, :]
        for r in range(1, R):
            total = total + weights[r] * grads[r, at, :]
        out_ref[at, :] = total

    @pl.loop(0, CHUNKS)
    def _(i):
        own_slab(i, False)
        relay(i, False)

        @pl.when(z != chip)
        def _():
            for n in range(4):
                line(order[n], i, False)

        @pl.when((z == chip) & (i == CHUNKS - 1))
        def _():
            line(order[3], i, False)

        for t in range(1, 4):
            express_on(t, i, False)

    y_sibling().wait_send()
    y_direct(0, via).wait_send()
    y_direct(1, other).wait_send()
    y_relay().wait_send()
    for n in (1, 2, 3):
        y_share(n).wait_send()
    for j in range(1, Z):
        around_z(j).wait_send()
    for j in range(1, R):
        around_plane(j).wait_send()


def by_tiles(R, Z, activations, out_grads):
    tokens, slab = activations.shape
    columns = out_grads.shape[1]
    width = slab * Z // R
    kept = -(-len(pair_list(R)) // 8) * 8
    dma = pltpu.SemaphoreType.DMA
    return pl.pallas_call(
        functools.partial(kernel, R, Z),
        out_shape=(
            jax.ShapeDtypeStruct((width, columns), jnp.float32),
            jax.ShapeDtypeStruct((Z, 2, width, tokens), jnp.bfloat16),
        ),
        in_specs=[pl.BlockSpec(memory_space=pl.ANY)] * 2,
        out_specs=(
            pl.BlockSpec(memory_space=pltpu.VMEM),
            pl.BlockSpec(memory_space=pl.ANY),
        ),
        scratch_shapes=[
            pltpu.VMEM((R, width, tokens), jnp.bfloat16),
            pltpu.VMEM((R, tokens, columns), jnp.bfloat16),
            pltpu.VMEM((R, width, columns), jnp.float32),
            pltpu.VMEM((2, kept, 128), jnp.float32),
            pltpu.VMEM((Z - 1, kept, 128), jnp.float32),
            pltpu.VMEM((R - 1, kept, 128), jnp.float32),
            dma((Z, CHUNKS)),
            dma((Z, CHUNKS)),
            dma((Z, CHUNKS, 2)),
            dma((R, CHUNKS)),
            dma((CHUNKS, 2)),
            dma((2, R, CHUNKS)),
            dma((3,)),
            dma((R,)),
            dma,
            dma((3,)),
            dma,
            dma((Z - 1,)),
            dma((Z - 1,)),
            dma((R - 1,)),
            dma((R - 1,)),
        ],
        compiler_params=pltpu.CompilerParams(
            collective_id=0, has_side_effects=True, vmem_limit_bytes=60 * 1024 * 1024
        ),
        cost_estimate=pl.CostEstimate(
            flops=2 * R * tokens * width * columns,
            bytes_accessed=2 * R * tokens * (width + columns),
            transcendentals=0,
        ),
    )(activations.T.reshape(2, width, tokens), out_grads)[0]


def solution(mesh):
    R, Z = mesh.shape["dp"], mesh.shape["tensor"]

    def on_device(activations, out_grads):
        tokens, slab = activations.shape
        columns = out_grads.shape[1]
        width = slab * Z // R
        fits = (
            R == 8 and Z == 4 and width % 128 == 0 and columns % 256 == 0
            and tokens % 128 == 0 and width % (CHUNKS * 16) == 0
            and R * (2 * tokens * (width + columns) + 4 * width * columns) < 50 * 2**20
        )
        if fits:
            return by_tiles(R, Z, activations, out_grads)
        return by_halving(activations, out_grads)

    return jax.shard_map(
        on_device,
        mesh=mesh,
        in_specs=(P("dp", "tensor"), P("dp", "tensor")),
        out_specs=P("dp", "tensor"),
        check_vma=False,
    )
```

```python
import functools
import jax
import jax.numpy as jnp
from jax import lax
from jax.experimental import pallas as pl
from jax.experimental.pallas import tpu as pltpu
from jax.sharding import PartitionSpec as P

epsilon = 1e-06
MESH = pl.DeviceIdType.MESH
CHUNKS = 8


def swapped(x, axis, apart):
    return lax.ppermute(x, axis, [(i, i ^ 1 << apart) for i in range(lax.axis_size(axis))])


def group_totals(partials, section):
    for bit_number in range(section + 1):
        partials = partials + swapped(partials, "dp", bit_number)
    return lax.psum(partials, "tensor")


def adasum_pair(mine, other, section, replica):
    upper_side = jnp.right_shift(replica, section) % 2 == 1
    mine_norm = jnp.sum(mine * mine)
    other_norm = jnp.sum(other * other)
    lower_norm = jnp.where(upper_side, other_norm, mine_norm)
    upper_norm = jnp.where(upper_side, mine_norm, other_norm)
    partials = jnp.stack([jnp.sum(mine * other), lower_norm, upper_norm])
    totals = group_totals(partials, section)
    lower_coef = 1.0 - totals[0] / (2.0 * (totals[1] + epsilon))
    upper_coef = 1.0 - totals[0] / (2.0 * (totals[2] + epsilon))
    mine_coef = jnp.where(upper_side, upper_coef, lower_coef)
    other_coef = jnp.where(upper_side, lower_coef, upper_coef)
    return mine_coef * mine + other_coef * other


def by_halving(activations, out_grads):
    replicas = lax.axis_size("dp")
    section_count = replicas.bit_length() - 1
    replica = lax.axis_index("dp")
    columns = out_grads.shape[1]
    slab_rows = activations.shape[1]
    block_rows = slab_rows * lax.axis_size("tensor") // replicas
    full_grad = jnp.einsum(
        "tk,tf->kf",
        lax.all_gather(activations, "tensor", axis=1, tiled=True),
        out_grads,
        preferred_element_type=jnp.float32,
    )
    holding = full_grad.reshape(replicas, block_rows, columns)
    for section in range(section_count):
        section_bit = jnp.right_shift(replica, section) % 2
        paired = holding.reshape(-1, 2, block_rows, columns)
        keeping = lax.dynamic_index_in_dim(paired, section_bit, axis=1, keepdims=False)
        sending = lax.dynamic_index_in_dim(paired, 1 - section_bit, axis=1, keepdims=False)
        received = swapped(sending, "dp", section)
        holding = adasum_pair(keeping, received, section, replica)
    return holding.reshape(block_rows, columns)


def pair_list(count):
    return [(a, b) for a in range(count) for b in range(a, count)]


def tree_weights(gram, count):
    weights = [[(r, None)] for r in range(count)]
    while count > 1:
        half = count // 2
        low, high = [], []
        for i in range(half):
            aa, bb, ab = gram[2 * i, 2 * i], gram[2 * i + 1, 2 * i + 1], gram[2 * i, 2 * i + 1]
            bound = jnp.sqrt(aa) * jnp.sqrt(bb)
            ab = jnp.clip(ab, -bound, bound)
            low.append(1.0 - ab / (2.0 * (aa + epsilon)))
            high.append(1.0 - ab / (2.0 * (bb + epsilon)))
        merged = {}
        for i, j in pair_list(half):
            cross = gram[2 * i, 2 * j + 1]
            back = gram[2 * i + 1, 2 * j] if i != j else cross
            value = (
                low[i] * (low[j] * gram[2 * i, 2 * j] + high[j] * cross)
                + high[i] * (low[j] * back + high[j] * gram[2 * i + 1, 2 * j + 1])
            )
            merged[i, j] = jnp.maximum(value, 0.0) if i == j else value
        weights = [
            [(r, low[i] if w is None else w * low[i]) for r, w in weights[2 * i]]
            + [(r, high[i] if w is None else w * high[i]) for r, w in weights[2 * i + 1]]
            for i in range(half)
        ]
        gram, count = merged, half
    return [w for _, w in sorted(weights[0], key=lambda item: item[0])]


def meet(R, Z, me, z):
    barrier = pltpu.get_barrier_semaphore()
    for j in range(1, Z):
        pl.semaphore_signal(barrier, inc=1, device_id=(me, (z + j) % Z), device_id_type=MESH)
    for j in range(1, R):
        pl.semaphore_signal(barrier, inc=1, device_id=((me + j) % R, z), device_id_type=MESH)
    pl.semaphore_wait(barrier, Z + R - 2)


def remote(src, dst, send, recv, device):
    return pltpu.make_async_remote_copy(
        src_ref=src, dst_ref=dst, send_sem=send, recv_sem=recv,
        device_id=device, device_id_type=MESH,
    )


def gather_kernel(
    R, Z, x_ref, y_ref, xg, yg, fw,
    esend, zrecv, xsend, xrecv, rsend, lsend, ysend, yrecv, psend, fsend, lsem,
):
    me = lax.axis_index("dp")
    z = lax.axis_index("tensor")
    chips = R // 2
    last = chips - 1
    chip, core = me // 2, me % 2
    sibling = chip * 2 + 1 - core
    width = xg.shape[1]
    rows = width // CHUNKS

    def across(c, way):
        return (c // 2) * 2 + 1 - c % 2 if way == 0 else (1 - c // 2) * 2 + c % 2

    side, above = across(chip, 0), across(chip, 1)
    opposite = across(side, 1)
    order = (chip, side, above, opposite)
    via = jnp.where(core == 0, side, above)
    other = jnp.where(core == 0, above, side)

    meet(R, Z, me, z)

    def go(copy, start):
        if start:
            copy.start()
        else:
            copy.wait_send()

    def span(i):
        return pl.ds(pl.multiple_of(i * rows, rows), rows)

    def held(s, i):
        return fw.at[s, :, span(i)]

    def to_owner(src, r, i, h, send, dest):
        return remote(src.at[h], xg.at[r, span(i)], send, xrecv.at[r, i], (dest, z))

    def express(src, s, i, start):
        @pl.when((chip == last) & (z < Z - 1))
        def _():
            go(remote(src, held(s, i), esend.at[s, i], zrecv.at[s, i], (me, z + 1)), start)

        @pl.when((chip == 0) & (z > 0))
        def _():
            go(remote(src, held(s, i), esend.at[s, i], zrecv.at[s, i], (me, z - 1)), start)

    def own_slab(i, start):
        src = x_ref.at[:, span(i)]
        express(src, z, i, start)

        @pl.when(z == chip)
        def _():
            for h in range(2):
                @pl.when(h == core)
                def _():
                    if start:
                        pltpu.make_async_copy(
                            src.at[h], xg.at[me, span(i)], xrecv.at[me, i]
                        ).start()

                @pl.when(h != core)
                def _():
                    go(to_owner(src, me, i, h, xsend.at[z, i, h], sibling), start)

        @pl.when((z == side) | (z == above))
        def _():
            for h in range(2):
                go(to_owner(src, me, i, h, xsend.at[z, i, h], 2 * z + h), start)

        @pl.when(z == opposite)
        def _():
            go(
                remote(src, held(z, i), xsend.at[z, i, 0], zrecv.at[z, i], (2 * via + core, z)),
                start,
            )

    def relay(i, start):
        @pl.when(z == other)
        def _():
            r = 2 * via + core
            if start:
                remote(held(z, i), held(z, i), rsend.at[i, 0], zrecv.at[z, i], (r, z)).wait_recv()
            for h in range(2):
                go(to_owner(held(z, i), r, i, h, rsend.at[i, h], 2 * z + h), start)

    def ways(o):
        return (
            (z >= chip) & (z < Z - 1) & (o != last),
            (z <= chip) & (z > 0) & (o != 0),
        )

    def x_arrived(r, i):
        pltpu.make_async_copy(xg.at[r, span(i)], xg.at[r, span(i)], xrecv.at[r, i]).wait()

    def line(o, i, start):
        right, left = ways(o)
        for k in range(2):
            r = 2 * o + k
            if start:
                @pl.when(right | left)
                def _():
                    x_arrived(r, i)
            for way, there in ((0, right), (1, left)):
                @pl.when(there)
                def _():
                    go(
                        remote(
                            xg.at[r, span(i)], xg.at[r, span(i)], lsend.at[way, r, i],
                            xrecv.at[r, i], (me, z + 1 - 2 * way),
                        ),
                        start,
                    )

    def express_on(t, i, start):
        for s, there in (
            (z - t, (chip == last) & (z - t >= 0)),
            (z + t, (chip == 0) & (z + t < Z)),
        ):
            @pl.when(there)
            def _():
                if start:
                    remote(held(s, i), held(s, i), esend.at[s, i], zrecv.at[s, i], (me, 0)).wait_recv()
                express(held(s, i), s, i, start)
                for h in range(2):
                    go(to_owner(held(s, i), me, i, h, xsend.at[s, i, h], 2 * s + h), start)

    def y_arrived(r):
        pltpu.make_async_copy(yg.at[r], yg.at[r], yrecv.at[r]).wait()

    def y_direct(n, c):
        return remote(y_ref, yg.at[me], ysend.at[n], yrecv.at[me], (2 * c + core, z))

    def y_sibling():
        return remote(y_ref, yg.at[me], ysend.at[2], yrecv.at[me], (sibling, z))

    def y_local():
        return pltpu.make_async_copy(y_ref, yg.at[me], lsem)

    def y_relay():
        r = 2 * via + core
        return remote(yg.at[r], yg.at[r], psend, yrecv.at[r], (2 * other + core, z))

    def y_share(n):
        r = 2 * order[n] + core
        return remote(yg.at[r], yg.at[r], fsend.at[n - 1], yrecv.at[r], (sibling, z))

    @pl.loop(0, CHUNKS)
    def _(i):
        own_slab(i, True)

    @pl.loop(0, CHUNKS)
    def _(i):
        line(order[0], i, True)
        relay(i, True)
        express_on(1, i, True)

        @pl.when(i == CHUNKS // 4)
        def _():
            y_sibling().start()
            y_direct(0, via).start()
            y_direct(1, other).start()
            y_local().start()

    y_local().wait()
    y_arrived(sibling)

    @pl.loop(0, CHUNKS)
    def _(i):
        line(order[1], i, True)
        express_on(2, i, True)

    y_arrived(2 * via + core)
    y_relay().start()
    y_arrived(2 * other + core)
    for n in (1, 2):
        y_share(n).start()

    @pl.loop(0, CHUNKS)
    def _(i):
        line(order[2], i, True)
        express_on(3, i, True)

    y_arrived(2 * opposite + core)
    y_share(3).start()

    @pl.loop(0, CHUNKS)
    def _(i):
        line(order[3], i, True)

    for o in (side, above, opposite):
        y_arrived(2 * o + 1 - core)

    @pl.loop(0, CHUNKS)
    def _(i):
        for o in order:
            right, left = ways(o)
            for k in range(2):
                @pl.when(jnp.logical_not(right | left))
                def _():
                    x_arrived(2 * o + k, i)

    @pl.loop(0, CHUNKS)
    def _(i):
        own_slab(i, False)
        relay(i, False)
        for n in range(4):
            line(order[n], i, False)
        for t in range(1, 4):
            express_on(t, i, False)

    y_sibling().wait_send()
    y_direct(0, via).wait_send()
    y_direct(1, other).wait_send()
    y_relay().wait_send()
    for n in (1, 2, 3):
        y_share(n).wait_send()

def combine_kernel(
    R, Z, x_ref, y_ref, out_ref,
    xg, yg, grads, part, first, second, xsem, ysem, asend, arecv, bsend, brecv,
):
    me = lax.axis_index("dp")
    z = lax.axis_index("tensor")
    width, columns = out_ref.shape
    tile = 256
    copies = [
        (
            pltpu.make_async_copy(x_ref.at[r], xg.at[r], xsem.at[r]),
            pltpu.make_async_copy(y_ref.at[r], yg.at[r], ysem.at[r]),
        )
        for r in range(R)
    ]
    for x_copy, y_copy in copies:
        x_copy.start()
        y_copy.start()

    meet(R, Z, me, z)

    for r in range(R):
        for copy in copies[r]:
            copy.wait()

        @pl.loop(0, columns // tile)
        def _(q):
            at = pl.ds(pl.multiple_of(q * tile, tile), tile)
            grads[r, :, at] = jnp.dot(
                xg[r], yg[r, :, at], preferred_element_type=jnp.float32
            )

    pairs = pair_list(R)

    def accumulate(b, sums):
        at = pl.ds(pl.multiple_of(b * 8, 8), 8)
        sums = list(sums)
        for q in range(columns // 128):
            blocks = [grads[r, at, pl.ds(q * 128, 128)] for r in range(R)]
            for n, (a, c) in enumerate(pairs):
                sums[n] = sums[n] + blocks[a] * blocks[c]
        return tuple(sums)

    sums = lax.fori_loop(
        0, width // 8, accumulate, tuple(jnp.zeros((8, 128), jnp.float32) for _ in pairs)
    )
    part[0] = jnp.zeros(part.shape[1:], jnp.float32)
    for n in range(len(pairs)):
        part[0, pl.ds(n, 1), :] = jnp.sum(sums[n], axis=0, keepdims=True)

    def around_z(j):
        return remote(part.at[0], first.at[j - 1], asend.at[j - 1], arecv.at[j - 1], (me, (z + j) % Z))

    def around_plane(j):
        return remote(
            part.at[1], second.at[j - 1], bsend.at[j - 1], brecv.at[j - 1], ((me + j) % R, z)
        )

    for j in range(1, Z):
        around_z(j).start()
    for j in range(1, Z):
        around_z(j).wait_recv()
    part[1] = part[0] + sum(first[j - 1] for j in range(1, Z))
    for j in range(1, R):
        around_plane(j).start()
    for j in range(1, R):
        around_plane(j).wait_recv()
    totals = part[1] + sum(second[j - 1] for j in range(1, R))
    totals = jnp.sum(totals, axis=1, keepdims=True)
    gram = {pair: totals[n:n + 1, :] for n, pair in enumerate(pairs)}
    weights = tree_weights(gram, R)

    band = 16

    @pl.loop(0, width // band)
    def _(b):
        at = pl.ds(pl.multiple_of(b * band, band), band)
        total = weights[0] * grads[0, at, :]
        for r in range(1, R):
            total = total + weights[r] * grads[r, at, :]
        out_ref[at, :] = total

    for j in range(1, Z):
        around_z(j).wait_send()
    for j in range(1, R):
        around_plane(j).wait_send()


def by_tiles(R, Z, activations, out_grads):
    tokens, slab = activations.shape
    columns = out_grads.shape[1]
    width = slab * Z // R
    kept = -(-len(pair_list(R)) // 8) * 8
    dma = pltpu.SemaphoreType.DMA
    anywhere = pl.BlockSpec(memory_space=pl.ANY)
    x_all, y_all, _ = pl.pallas_call(
        functools.partial(gather_kernel, R, Z),
        out_shape=(
            jax.ShapeDtypeStruct((R, width, tokens), jnp.bfloat16),
            jax.ShapeDtypeStruct((R, tokens, columns), jnp.bfloat16),
            jax.ShapeDtypeStruct((Z, 2, width, tokens), jnp.bfloat16),
        ),
        in_specs=[anywhere] * 2,
        out_specs=(anywhere,) * 3,
        scratch_shapes=[
            dma((Z, CHUNKS)),
            dma((Z, CHUNKS)),
            dma((Z, CHUNKS, 2)),
            dma((R, CHUNKS)),
            dma((CHUNKS, 2)),
            dma((2, R, CHUNKS)),
            dma((3,)),
            dma((R,)),
            dma,
            dma((3,)),
            dma,
        ],
        compiler_params=pltpu.CompilerParams(
            collective_id=0, has_side_effects=True, vmem_limit_bytes=60 * 1024 * 1024
        ),
        name="gather_inputs",
    )(activations.T.reshape(2, width, tokens), out_grads)
    return pl.pallas_call(
        functools.partial(combine_kernel, R, Z),
        out_shape=jax.ShapeDtypeStruct((width, columns), jnp.float32),
        in_specs=[anywhere] * 2,
        out_specs=pl.BlockSpec(memory_space=pltpu.VMEM),
        scratch_shapes=[
            pltpu.VMEM((R, width, tokens), jnp.bfloat16),
            pltpu.VMEM((R, tokens, columns), jnp.bfloat16),
            pltpu.VMEM((R, width, columns), jnp.float32),
            pltpu.VMEM((2, kept, 128), jnp.float32),
            pltpu.VMEM((Z - 1, kept, 128), jnp.float32),
            pltpu.VMEM((R - 1, kept, 128), jnp.float32),
            dma((R,)),
            dma((R,)),
            dma((Z - 1,)),
            dma((Z - 1,)),
            dma((R - 1,)),
            dma((R - 1,)),
        ],
        compiler_params=pltpu.CompilerParams(
            collective_id=1, has_side_effects=True, vmem_limit_bytes=60 * 1024 * 1024
        ),
        name="combine",
    )(x_all, y_all)


def solution(mesh):
    R, Z = mesh.shape["dp"], mesh.shape["tensor"]

    def on_device(activations, out_grads):
        tokens, slab = activations.shape
        columns = out_grads.shape[1]
        width = slab * Z // R
        fits = (
            R == 8 and Z == 4 and width % 128 == 0 and columns % 256 == 0
            and tokens % 128 == 0 and width % (CHUNKS * 16) == 0
            and R * (2 * tokens * (width + columns) + 4 * width * columns) < 50 * 2**20
        )
        if fits:
            return by_tiles(R, Z, activations, out_grads)
        return by_halving(activations, out_grads)

    return jax.shard_map(
        on_device,
        mesh=mesh,
        in_specs=(P("dp", "tensor"), P("dp", "tensor")),
        out_specs=P("dp", "tensor"),
        check_vma=False,
    )
```

```python
import functools
import jax
import jax.numpy as jnp
from jax import lax
from jax.experimental import pallas as pl
from jax.experimental.pallas import tpu as pltpu
from jax.sharding import PartitionSpec as P

epsilon = 1e-06
MESH = pl.DeviceIdType.MESH
CHUNKS = 10
FOLD = 5


def swapped(x, axis, apart):
    return lax.ppermute(x, axis, [(i, i ^ 1 << apart) for i in range(lax.axis_size(axis))])


def group_totals(partials, section):
    for bit_number in range(section + 1):
        partials = partials + swapped(partials, "dp", bit_number)
    return lax.psum(partials, "tensor")


def adasum_pair(mine, other, section, replica):
    upper_side = jnp.right_shift(replica, section) % 2 == 1
    mine_norm = jnp.sum(mine * mine)
    other_norm = jnp.sum(other * other)
    lower_norm = jnp.where(upper_side, other_norm, mine_norm)
    upper_norm = jnp.where(upper_side, mine_norm, other_norm)
    partials = jnp.stack([jnp.sum(mine * other), lower_norm, upper_norm])
    totals = group_totals(partials, section)
    lower_coef = 1.0 - totals[0] / (2.0 * (totals[1] + epsilon))
    upper_coef = 1.0 - totals[0] / (2.0 * (totals[2] + epsilon))
    mine_coef = jnp.where(upper_side, upper_coef, lower_coef)
    other_coef = jnp.where(upper_side, lower_coef, upper_coef)
    return mine_coef * mine + other_coef * other


def by_halving(activations, out_grads):
    replicas = lax.axis_size("dp")
    section_count = replicas.bit_length() - 1
    replica = lax.axis_index("dp")
    columns = out_grads.shape[1]
    slab_rows = activations.shape[1]
    block_rows = slab_rows * lax.axis_size("tensor") // replicas
    full_grad = jnp.einsum(
        "tk,tf->kf",
        lax.all_gather(activations, "tensor", axis=1, tiled=True),
        out_grads,
        preferred_element_type=jnp.float32,
    )
    holding = full_grad.reshape(replicas, block_rows, columns)
    for section in range(section_count):
        section_bit = jnp.right_shift(replica, section) % 2
        paired = holding.reshape(-1, 2, block_rows, columns)
        keeping = lax.dynamic_index_in_dim(paired, section_bit, axis=1, keepdims=False)
        sending = lax.dynamic_index_in_dim(paired, 1 - section_bit, axis=1, keepdims=False)
        received = swapped(sending, "dp", section)
        holding = adasum_pair(keeping, received, section, replica)
    return holding.reshape(block_rows, columns)


def pair_list(count):
    return [(a, b) for a in range(count) for b in range(a, count)]


def tree_weights(gram, count):
    weights = [[(r, None)] for r in range(count)]
    while count > 1:
        half = count // 2
        low, high = [], []
        for i in range(half):
            aa, bb, ab = gram[2 * i, 2 * i], gram[2 * i + 1, 2 * i + 1], gram[2 * i, 2 * i + 1]
            bound = jnp.sqrt(aa) * jnp.sqrt(bb)
            ab = jnp.clip(ab, -bound, bound)
            low.append(1.0 - ab / (2.0 * (aa + epsilon)))
            high.append(1.0 - ab / (2.0 * (bb + epsilon)))
        merged = {}
        for i, j in pair_list(half):
            cross = gram[2 * i, 2 * j + 1]
            back = gram[2 * i + 1, 2 * j] if i != j else cross
            value = (
                low[i] * (low[j] * gram[2 * i, 2 * j] + high[j] * cross)
                + high[i] * (low[j] * back + high[j] * gram[2 * i + 1, 2 * j + 1])
            )
            merged[i, j] = jnp.maximum(value, 0.0) if i == j else value
        weights = [
            [(r, low[i] if w is None else w * low[i]) for r, w in weights[2 * i]]
            + [(r, high[i] if w is None else w * high[i]) for r, w in weights[2 * i + 1]]
            for i in range(half)
        ]
        gram, count = merged, half
    return [w for _, w in sorted(weights[0], key=lambda item: item[0])]


def kernel(
    R, Z, x_ref, y_ref, out_ref, fw,
    xg, yg, grads, part, first, second,
    esend, zrecv, xsend, xrecv, rsend, lsend, ysend, yrecv, fsend, lsem,
    asend, arecv, bsend, brecv,
):
    me = lax.axis_index("dp")
    z = lax.axis_index("tensor")
    chips = R // 2
    last = chips - 1
    chip, core = me // 2, me % 2
    sibling = chip * 2 + 1 - core
    width = xg.shape[1]
    rows = width // CHUNKS
    columns = yg.shape[2]

    def across(c, way):
        return (c // 2) * 2 + 1 - c % 2 if way == 0 else (1 - c // 2) * 2 + c % 2

    side, above = across(chip, 0), across(chip, 1)
    opposite = across(side, 1)
    order = (chip, side, above, opposite)
    via = jnp.where(core == 0, side, above)
    other = jnp.where(core == 0, above, side)

    barrier = pltpu.get_barrier_semaphore()
    for j in range(1, Z):
        pl.semaphore_signal(barrier, inc=1, device_id=(me, (z + j) % Z), device_id_type=MESH)
    for j in range(1, R):
        pl.semaphore_signal(barrier, inc=1, device_id=((me + j) % R, z), device_id_type=MESH)
    pl.semaphore_wait(barrier, Z + R - 2)

    def remote(src, dst, send, recv, device):
        return pltpu.make_async_remote_copy(
            src_ref=src, dst_ref=dst, send_sem=send, recv_sem=recv,
            device_id=device, device_id_type=MESH,
        )

    def go(copy, start):
        if start:
            copy.start()
        else:
            copy.wait_send()

    def span(i):
        return pl.ds(pl.multiple_of(i * rows, rows), rows)

    def held(s, i):
        return fw.at[s, :, span(i)]

    def to_owner(src, r, i, h, send, dest):
        return remote(src.at[h], xg.at[r, span(i)], send, xrecv.at[r, i], (dest, z))

    def express(src, s, i, start):
        @pl.when((chip == last) & (z < Z - 1))
        def _():
            go(remote(src, held(s, i), esend.at[s, i], zrecv.at[s, i], (me, z + 1)), start)

        @pl.when((chip == 0) & (z > 0))
        def _():
            go(remote(src, held(s, i), esend.at[s, i], zrecv.at[s, i], (me, z - 1)), start)

    def own_slab(i, start):
        src = x_ref.at[:, span(i)]

        @pl.when(z == chip)
        def _():
            for h in range(2):
                @pl.when(h == core)
                def _():
                    if start:
                        pltpu.make_async_copy(
                            src.at[h], xg.at[me, span(i)], xrecv.at[me, i]
                        ).start()

                @pl.when(h != core)
                def _():
                    go(to_owner(src, me, i, h, xsend.at[z, i, h], sibling), start)

        @pl.when((z == side) | (z == above))
        def _():
            for h in range(2):
                go(to_owner(src, me, i, h, xsend.at[z, i, h], 2 * z + h), start)

        @pl.when(z == opposite)
        def _():
            go(
                remote(src, held(z, i), xsend.at[z, i, 0], zrecv.at[z, i], (2 * via + core, z)),
                start,
            )

    def relay(i, start):
        @pl.when(z == other)
        def _():
            r = 2 * via + core
            if start:
                remote(held(z, i), held(z, i), rsend.at[i, 0], zrecv.at[z, i], (r, z)).wait_recv()
            for h in range(2):
                go(to_owner(held(z, i), r, i, h, rsend.at[i, h], 2 * z + h), start)

    def ways(o):
        return (
            (z >= chip) & (z < Z - 1) & (o != last),
            (z <= chip) & (z > 0) & (o != 0),
        )

    def x_arrived(r, i):
        pltpu.make_async_copy(xg.at[r, span(i)], xg.at[r, span(i)], xrecv.at[r, i]).wait()

    def line(o, i, start):
        right, left = ways(o)
        for k in range(2):
            r = 2 * o + k
            if start:
                @pl.when(right | left)
                def _():
                    x_arrived(r, i)
            for way, there in ((0, right), (1, left)):
                @pl.when(there)
                def _():
                    go(
                        remote(
                            xg.at[r, span(i)], xg.at[r, span(i)], lsend.at[way, r, i],
                            xrecv.at[r, i], (me, z + 1 - 2 * way),
                        ),
                        start,
                    )

    def pace(members, i):
        @pl.when((z == chip) & (i > 0))
        def _():
            for o in members:
                line(o, i - 1, False)

    def drain(members):
        @pl.when(z == chip)
        def _():
            for o in members:
                line(o, CHUNKS - 1, False)

    def express_on(t, i, start):
        for s, there in (
            (z - t, (chip == last) & (z - t >= 0)),
            (z + t, (chip == 0) & (z + t < Z)),
        ):
            @pl.when(there)
            def _():
                if start:
                    remote(held(s, i), held(s, i), esend.at[s, i], zrecv.at[s, i], (me, 0)).wait_recv()
                express(held(s, i), s, i, start)
                for h in range(2):
                    go(to_owner(held(s, i), me, i, h, xsend.at[s, i, h], 2 * s + h), start)

    def y_arrived(r):
        pltpu.make_async_copy(yg.at[r], yg.at[r], yrecv.at[r]).wait()

    def y_direct(n):
        return remote(
            y_ref, yg.at[me], ysend.at[n], yrecv.at[me], (2 * order[n] + core, z)
        )

    def y_sibling():
        return remote(y_ref, yg.at[me], ysend.at[0], yrecv.at[me], (sibling, z))

    def y_local():
        return pltpu.make_async_copy(y_ref, yg.at[me], lsem)

    def y_share(n):
        r = 2 * order[n] + core
        return remote(yg.at[r], yg.at[r], fsend.at[n - 1], yrecv.at[r], (sibling, z))

    tile = 256
    units = CHUNKS // FOLD

    def product(o, u):
        right, left = ways(o)
        for k in range(2):
            r = 2 * o + k

            @pl.when(jnp.logical_not(right | left))
            def _():
                for f in range(FOLD):
                    x_arrived(r, u * FOLD + f)

            block = pl.ds(pl.multiple_of(u * FOLD * rows, FOLD * rows), FOLD * rows)

            @pl.loop(0, columns // tile)
            def _(q):
                at = pl.ds(pl.multiple_of(q * tile, tile), tile)
                grads[r, block, at] = jnp.dot(
                    xg[r, block, :], yg[r, :, at], preferred_element_type=jnp.float32
                )

    @pl.loop(0, CHUNKS)
    def _(i):
        own_slab(i, True)

    @pl.loop(0, CHUNKS)
    def _(i):
        express(x_ref.at[:, span(i)], z, i, True)
        line(chip, i, True)
        express_on(1, i, True)
        pace((chip,), i)

        @pl.when(i >= CHUNKS // 2)
        def _():
            relay(2 * i - CHUNKS, True)
            relay(2 * i - CHUNKS + 1, True)

    y_sibling().start()
    y_local().start()
    for n in (1, 2, 3):
        y_direct(n).start()

    @pl.loop(0, CHUNKS)
    def _(i):
        line(side, i, True)
        line(above, i, True)

        @pl.when(i == 0)
        def _():
            drain((chip,))

        for f in range(2):
            m = 2 * i + f
            for t in range(2, Z):
                @pl.when(m // CHUNKS == t - 2)
                def _():
                    express_on(t, m % CHUNKS, True)

        pace((side, above), i)

        @pl.when(i == CHUNKS - units)
        def _():
            y_local().wait()
            y_arrived(sibling)

        @pl.when(i >= CHUNKS - units)
        def _():
            product(chip, i - (CHUNKS - units))

    @pl.loop(0, CHUNKS)
    def _(i):
        line(opposite, i, True)

        @pl.when(i == 0)
        def _():
            drain((side, above))

        pace((opposite,), i)

    for n in (1, 2, 3):
        y_arrived(2 * order[n] + core)
        y_share(n).start()

    for n in (1, 2, 3):
        y_arrived(2 * order[n] + 1 - core)

        @pl.loop(0, units)
        def _(u):
            product(order[n], u)

    pairs = pair_list(R)

    def accumulate(b, sums):
        at = pl.ds(pl.multiple_of(b * 8, 8), 8)
        sums = list(sums)
        for q in range(columns // 128):
            blocks = [grads[r, at, pl.ds(q * 128, 128)] for r in range(R)]
            for n, (a, c) in enumerate(pairs):
                sums[n] = sums[n] + blocks[a] * blocks[c]
        return tuple(sums)

    sums = lax.fori_loop(
        0, width // 8, accumulate, tuple(jnp.zeros((8, 128), jnp.float32) for _ in pairs)
    )
    part[0] = jnp.zeros(part.shape[1:], jnp.float32)
    for n in range(len(pairs)):
        part[0, pl.ds(n, 1), :] = jnp.sum(sums[n], axis=0, keepdims=True)

    def around_z(j):
        return remote(part.at[0], first.at[j - 1], asend.at[j - 1], arecv.at[j - 1], (me, (z + j) % Z))

    def around_plane(j):
        return remote(
            part.at[1], second.at[j - 1], bsend.at[j - 1], brecv.at[j - 1], ((me + j) % R, z)
        )

    for j in range(1, Z):
        around_z(j).start()
    for j in range(1, Z):
        around_z(j).wait_recv()
    part[1] = part[0] + sum(first[j - 1] for j in range(1, Z))
    for j in range(1, R):
        around_plane(j).start()
    for j in range(1, R):
        around_plane(j).wait_recv()
    totals = part[1] + sum(second[j - 1] for j in range(1, R))
    totals = jnp.sum(totals, axis=1, keepdims=True)
    gram = {pair: totals[n:n + 1, :] for n, pair in enumerate(pairs)}
    weights = tree_weights(gram, R)

    band = 16

    @pl.loop(0, width // band)
    def _(b):
        at = pl.ds(pl.multiple_of(b * band, band), band)
        total = weights[0] * grads[0, at, :]
        for r in range(1, R):
            total = total + weights[r] * grads[r, at, :]
        out_ref[at, :] = total

    @pl.loop(0, CHUNKS)
    def _(i):
        own_slab(i, False)
        express(x_ref.at[:, span(i)], z, i, False)
        relay(i, False)
        for t in range(1, Z):
            express_on(t, i, False)

        @pl.when(z != chip)
        def _():
            for o in order:
                line(o, i, False)

    drain((opposite,))
    y_sibling().wait_send()
    for n in (1, 2, 3):
        y_direct(n).wait_send()
        y_share(n).wait_send()
    for j in range(1, Z):
        around_z(j).wait_send()
    for j in range(1, R):
        around_plane(j).wait_send()


def by_tiles(R, Z, activations, out_grads):
    tokens, slab = activations.shape
    columns = out_grads.shape[1]
    width = slab * Z // R
    kept = -(-len(pair_list(R)) // 8) * 8
    dma = pltpu.SemaphoreType.DMA
    return pl.pallas_call(
        functools.partial(kernel, R, Z),
        out_shape=(
            jax.ShapeDtypeStruct((width, columns), jnp.float32),
            jax.ShapeDtypeStruct((Z, 2, width, tokens), jnp.bfloat16),
        ),
        in_specs=[pl.BlockSpec(memory_space=pl.ANY)] * 2,
        out_specs=(
            pl.BlockSpec(memory_space=pltpu.VMEM),
            pl.BlockSpec(memory_space=pl.ANY),
        ),
        scratch_shapes=[
            pltpu.VMEM((R, width, tokens), jnp.bfloat16),
            pltpu.VMEM((R, tokens, columns), jnp.bfloat16),
            pltpu.VMEM((R, width, columns), jnp.float32),
            pltpu.VMEM((2, kept, 128), jnp.float32),
            pltpu.VMEM((Z - 1, kept, 128), jnp.float32),
            pltpu.VMEM((R - 1, kept, 128), jnp.float32),
            dma((Z, CHUNKS)),
            dma((Z, CHUNKS)),
            dma((Z, CHUNKS, 2)),
            dma((R, CHUNKS)),
            dma((CHUNKS, 2)),
            dma((2, R, CHUNKS)),
            dma((4,)),
            dma((R,)),
            dma((3,)),
            dma,
            dma((Z - 1,)),
            dma((Z - 1,)),
            dma((R - 1,)),
            dma((R - 1,)),
        ],
        compiler_params=pltpu.CompilerParams(
            collective_id=0, has_side_effects=True, vmem_limit_bytes=60 * 1024 * 1024
        ),
        cost_estimate=pl.CostEstimate(
            flops=2 * R * tokens * width * columns,
            bytes_accessed=2 * R * tokens * (width + columns),
            transcendentals=0,
        ),
    )(activations.T.reshape(2, width, tokens), out_grads)[0]


def solution(mesh):
    R, Z = mesh.shape["dp"], mesh.shape["tensor"]

    def on_device(activations, out_grads):
        tokens, slab = activations.shape
        columns = out_grads.shape[1]
        width = slab * Z // R
        fits = (
            R == 8 and Z == 4 and width % 128 == 0 and columns % 256 == 0
            and tokens % 128 == 0 and width % (CHUNKS * 16) == 0
            and R * (2 * tokens * (width + columns) + 4 * width * columns) < 50 * 2**20
        )
        if fits:
            return by_tiles(R, Z, activations, out_grads)
        return by_halving(activations, out_grads)

    return jax.shard_map(
        on_device,
        mesh=mesh,
        in_specs=(P("dp", "tensor"), P("dp", "tensor")),
        out_specs=P("dp", "tensor"),
        check_vma=False,
    )
```

```python
import functools
import jax
import jax.numpy as jnp
from jax import lax
from jax.experimental import pallas as pl
from jax.experimental.pallas import tpu as pltpu
from jax.sharding import PartitionSpec as P

epsilon = 1e-06
MESH = pl.DeviceIdType.MESH
CHUNKS = 8
FOLD = 4


def swapped(x, axis, apart):
    return lax.ppermute(x, axis, [(i, i ^ 1 << apart) for i in range(lax.axis_size(axis))])


def group_totals(partials, section):
    for bit_number in range(section + 1):
        partials = partials + swapped(partials, "dp", bit_number)
    return lax.psum(partials, "tensor")


def adasum_pair(mine, other, section, replica):
    upper_side = jnp.right_shift(replica, section) % 2 == 1
    mine_norm = jnp.sum(mine * mine)
    other_norm = jnp.sum(other * other)
    lower_norm = jnp.where(upper_side, other_norm, mine_norm)
    upper_norm = jnp.where(upper_side, mine_norm, other_norm)
    partials = jnp.stack([jnp.sum(mine * other), lower_norm, upper_norm])
    totals = group_totals(partials, section)
    lower_coef = 1.0 - totals[0] / (2.0 * (totals[1] + epsilon))
    upper_coef = 1.0 - totals[0] / (2.0 * (totals[2] + epsilon))
    mine_coef = jnp.where(upper_side, upper_coef, lower_coef)
    other_coef = jnp.where(upper_side, lower_coef, upper_coef)
    return mine_coef * mine + other_coef * other


def by_halving(activations, out_grads):
    replicas = lax.axis_size("dp")
    section_count = replicas.bit_length() - 1
    replica = lax.axis_index("dp")
    columns = out_grads.shape[1]
    slab_rows = activations.shape[1]
    block_rows = slab_rows * lax.axis_size("tensor") // replicas
    full_grad = jnp.einsum(
        "tk,tf->kf",
        lax.all_gather(activations, "tensor", axis=1, tiled=True),
        out_grads,
        preferred_element_type=jnp.float32,
    )
    holding = full_grad.reshape(replicas, block_rows, columns)
    for section in range(section_count):
        section_bit = jnp.right_shift(replica, section) % 2
        paired = holding.reshape(-1, 2, block_rows, columns)
        keeping = lax.dynamic_index_in_dim(paired, section_bit, axis=1, keepdims=False)
        sending = lax.dynamic_index_in_dim(paired, 1 - section_bit, axis=1, keepdims=False)
        received = swapped(sending, "dp", section)
        holding = adasum_pair(keeping, received, section, replica)
    return holding.reshape(block_rows, columns)


def pair_list(count):
    return [(a, b) for a in range(count) for b in range(a, count)]


def tree_weights(gram, count):
    weights = [[(r, None)] for r in range(count)]
    while count > 1:
        half = count // 2
        low, high = [], []
        for i in range(half):
            aa, bb, ab = gram[2 * i, 2 * i], gram[2 * i + 1, 2 * i + 1], gram[2 * i, 2 * i + 1]
            bound = jnp.sqrt(aa) * jnp.sqrt(bb)
            ab = jnp.clip(ab, -bound, bound)
            low.append(1.0 - ab / (2.0 * (aa + epsilon)))
            high.append(1.0 - ab / (2.0 * (bb + epsilon)))
        merged = {}
        for i, j in pair_list(half):
            cross = gram[2 * i, 2 * j + 1]
            back = gram[2 * i + 1, 2 * j] if i != j else cross
            value = (
                low[i] * (low[j] * gram[2 * i, 2 * j] + high[j] * cross)
                + high[i] * (low[j] * back + high[j] * gram[2 * i + 1, 2 * j + 1])
            )
            merged[i, j] = jnp.maximum(value, 0.0) if i == j else value
        weights = [
            [(r, low[i] if w is None else w * low[i]) for r, w in weights[2 * i]]
            + [(r, high[i] if w is None else w * high[i]) for r, w in weights[2 * i + 1]]
            for i in range(half)
        ]
        gram, count = merged, half
    return [w for _, w in sorted(weights[0], key=lambda item: item[0])]


def kernel(
    R, Z, x_ref, y_ref, out_ref, fw,
    xg, yg, grads, part, first, second,
    zsend, zrecv, xsend, xrecv, ysend, yrecv, fsend, lsem, asend, arecv, bsend, brecv,
):
    me = lax.axis_index("dp")
    z = lax.axis_index("tensor")
    chips = R // 2
    chip, core = me // 2, me % 2
    sibling = chip * 2 + 1 - core
    width = xg.shape[1]
    rows = width // CHUNKS
    columns = yg.shape[2]

    barrier = pltpu.get_barrier_semaphore()
    for j in range(1, Z):
        pl.semaphore_signal(barrier, inc=1, device_id=(me, (z + j) % Z), device_id_type=MESH)
    for j in range(1, R):
        pl.semaphore_signal(barrier, inc=1, device_id=((me + j) % R, z), device_id_type=MESH)
    pl.semaphore_wait(barrier, Z + R - 2)

    def remote(src, dst, send, recv, device):
        return pltpu.make_async_remote_copy(
            src_ref=src, dst_ref=dst, send_sem=send, recv_sem=recv,
            device_id=device, device_id_type=MESH,
        )

    def span(i):
        return pl.ds(pl.multiple_of(i * rows, rows), rows)

    def z_copy(src, s, i, way):
        to = z + 1 if way == 0 else z - 1
        return remote(
            src, fw.at[s, :, span(i)], zsend.at[way, s, i], zrecv.at[s, i], (me, to)
        )

    def own(i):
        return x_ref.at[:, span(i)]

    def held(s, i):
        return fw.at[s, :, span(i)]

    def scatter(src, s, i, start):
        for h in range(2):
            dest = 2 * s + h
            piece = src.at[h]

            @pl.when(dest == me)
            def _():
                if start:
                    pltpu.make_async_copy(piece, xg.at[me, span(i)], xrecv.at[me, i]).start()

            @pl.when(dest != me)
            def _():
                copy = remote(
                    piece, xg.at[me, span(i)], xsend.at[s, i, h], xrecv.at[me, i], (dest, z)
                )
                if start:
                    copy.start()
                else:
                    copy.wait_send()

    def move_along(start):
        @pl.loop(0, CHUNKS)
        def _(i):
            for way, there in ((0, z < Z - 1), (1, z > 0)):
                @pl.when(there)
                def _():
                    copy = z_copy(own(i), z, i, way)
                    if start:
                        copy.start()
                    else:
                        copy.wait_send()
            scatter(own(i), z, i, start)

        if start:
            send_out_grads()

        for t in range(1, Z):
            @pl.loop(0, CHUNKS)
            def _(i):
                for way, s, exists, further in (
                    (0, z - t, z - t >= 0, z < Z - 1),
                    (1, z + t, z + t < Z, z > 0),
                ):
                    @pl.when(exists)
                    def _():
                        if start:
                            z_copy(held(s, i), s, i, way).wait_recv()

                        @pl.when(further)
                        def _():
                            copy = z_copy(held(s, i), s, i, way)
                            if start:
                                copy.start()
                            else:
                                copy.wait_send()
                        scatter(held(s, i), s, i, start)


    def y_copy(j):
        return remote(
            y_ref, yg.at[me], ysend.at[j], yrecv.at[me], (((chip + j) % chips) * 2 + core, z)
        )

    def sibling_copy():
        return remote(y_ref, yg.at[me], ysend.at[0], yrecv.at[me], (sibling, z))

    def share_copy(j):
        r = ((chip + j) % chips) * 2 + core
        return remote(yg.at[r], yg.at[r], fsend.at[j], yrecv.at[r], (sibling, z))

    def local_y():
        return pltpu.make_async_copy(y_ref, yg.at[me], lsem)

    def send_out_grads():
        for j in range(1, chips):
            y_copy(j).start()
        sibling_copy().start()
        local_y().start()

    def share_out_grads():
        for j in range(1, chips):
            r = ((chip + j) % chips) * 2 + core
            remote(yg.at[r], yg.at[r], fsend.at[j], yrecv.at[r], (sibling, z)).wait_recv()
            share_copy(j).start()

    move_along(True)
    share_out_grads()

    local_y().wait()
    for j in range(chips):
        r = ((chip + j) % chips) * 2 + 1 - core
        remote(yg.at[r], yg.at[r], fsend.at[j], yrecv.at[r], (sibling, z)).wait_recv()

    tile = 256

    @pl.loop(0, CHUNKS // FOLD)
    def _(u):
        @pl.loop(0, R)
        def _(r):
            for f in range(FOLD):
                i = u * FOLD + f
                pltpu.make_async_copy(xg.at[r, span(i)], xg.at[r, span(i)], xrecv.at[r, i]).wait()

            block = pl.ds(pl.multiple_of(u * FOLD * rows, FOLD * rows), FOLD * rows)

            @pl.loop(0, columns // tile)
            def _(q):
                at = pl.ds(pl.multiple_of(q * tile, tile), tile)
                grads[r, block, at] = jnp.dot(
                    xg[r, block, :], yg[r, :, at], preferred_element_type=jnp.float32
                )

    pairs = pair_list(R)

    def accumulate(b, sums):
        at = pl.ds(pl.multiple_of(b * 8, 8), 8)
        sums = list(sums)
        for q in range(columns // 128):
            blocks = [grads[r, at, pl.ds(q * 128, 128)] for r in range(R)]
            for n, (a, c) in enumerate(pairs):
                sums[n] = sums[n] + blocks[a] * blocks[c]
        return tuple(sums)

    sums = lax.fori_loop(
        0, width // 8, accumulate, tuple(jnp.zeros((8, 128), jnp.float32) for _ in pairs)
    )
    part[0] = jnp.zeros(part.shape[1:], jnp.float32)
    for n in range(len(pairs)):
        part[0, pl.ds(n, 1), :] = jnp.sum(sums[n], axis=0, keepdims=True)

    def around_z(j):
        return remote(part.at[0], first.at[j - 1], asend.at[j - 1], arecv.at[j - 1], (me, (z + j) % Z))

    def around_plane(j):
        return remote(
            part.at[1], second.at[j - 1], bsend.at[j - 1], brecv.at[j - 1], ((me + j) % R, z)
        )

    for j in range(1, Z):
        around_z(j).start()
    for j in range(1, Z):
        around_z(j).wait_recv()
    part[1] = part[0] + sum(first[j - 1] for j in range(1, Z))
    for j in range(1, R):
        around_plane(j).start()
    for j in range(1, R):
        around_plane(j).wait_recv()
    totals = part[1] + sum(second[j - 1] for j in range(1, R))
    totals = jnp.sum(totals, axis=1, keepdims=True)
    gram = {pair: totals[n:n + 1, :] for n, pair in enumerate(pairs)}
    weights = tree_weights(gram, R)

    band = 16

    @pl.loop(0, width // band)
    def _(b):
        at = pl.ds(pl.multiple_of(b * band, band), band)
        total = weights[0] * grads[0, at, :]
        for r in range(1, R):
            total = total + weights[r] * grads[r, at, :]
        out_ref[at, :] = total

    move_along(False)
    for j in range(1, chips):
        y_copy(j).wait_send()
        share_copy(j).wait_send()
    sibling_copy().wait_send()
    for j in range(1, Z):
        around_z(j).wait_send()
    for j in range(1, R):
        around_plane(j).wait_send()


def by_tiles(R, Z, activations, out_grads):
    tokens, slab = activations.shape
    columns = out_grads.shape[1]
    width = slab * Z // R
    kept = -(-len(pair_list(R)) // 8) * 8
    dma = pltpu.SemaphoreType.DMA
    return pl.pallas_call(
        functools.partial(kernel, R, Z),
        out_shape=(
            jax.ShapeDtypeStruct((width, columns), jnp.float32),
            jax.ShapeDtypeStruct((Z, 2, width, tokens), jnp.bfloat16),
        ),
        in_specs=[pl.BlockSpec(memory_space=pl.ANY)] * 2,
        out_specs=(
            pl.BlockSpec(memory_space=pltpu.VMEM),
            pl.BlockSpec(memory_space=pl.ANY),
        ),
        scratch_shapes=[
            pltpu.VMEM((R, width, tokens), jnp.bfloat16),
            pltpu.VMEM((R, tokens, columns), jnp.bfloat16),
            pltpu.VMEM((R, width, columns), jnp.float32),
            pltpu.VMEM((2, kept, 128), jnp.float32),
            pltpu.VMEM((Z - 1, kept, 128), jnp.float32),
            pltpu.VMEM((R - 1, kept, 128), jnp.float32),
            dma((2, Z, CHUNKS)),
            dma((Z, CHUNKS)),
            dma((Z, CHUNKS, 2)),
            dma((R, CHUNKS)),
            dma((R // 2,)),
            dma((R,)),
            dma((R // 2,)),
            dma,
            dma((Z - 1,)),
            dma((Z - 1,)),
            dma((R - 1,)),
            dma((R - 1,)),
        ],
        compiler_params=pltpu.CompilerParams(
            collective_id=0, has_side_effects=True, vmem_limit_bytes=60 * 1024 * 1024
        ),
        cost_estimate=pl.CostEstimate(
            flops=2 * R * tokens * width * columns,
            bytes_accessed=2 * R * tokens * (width + columns),
            transcendentals=0,
        ),
    )(activations.T.reshape(2, width, tokens), out_grads)[0]


def solution(mesh):
    R, Z = mesh.shape["dp"], mesh.shape["tensor"]

    def on_device(activations, out_grads):
        tokens, slab = activations.shape
        columns = out_grads.shape[1]
        width = slab * Z // R
        fits = (
            R == 8 and Z == 4 and width % 128 == 0 and columns % 256 == 0
            and tokens % 128 == 0 and width % (CHUNKS * 16) == 0
            and R * (2 * tokens * (width + columns) + 4 * width * columns) < 50 * 2**20
        )
        if fits:
            return by_tiles(R, Z, activations, out_grads)
        return by_halving(activations, out_grads)

    return jax.shard_map(
        on_device,
        mesh=mesh,
        in_specs=(P("dp", "tensor"), P("dp", "tensor")),
        out_specs=P("dp", "tensor"),
        check_vma=False,
    )
```

```python
import functools
import jax
import jax.numpy as jnp
from jax import lax
from jax.experimental import pallas as pl
from jax.experimental.pallas import tpu as pltpu
from jax.sharding import PartitionSpec as P

epsilon = 1e-06
MESH = pl.DeviceIdType.MESH
CHUNKS = 8
FOLD = 4
LAG = 2


def swapped(x, axis, apart):
    return lax.ppermute(x, axis, [(i, i ^ 1 << apart) for i in range(lax.axis_size(axis))])


def group_totals(partials, section):
    for bit_number in range(section + 1):
        partials = partials + swapped(partials, "dp", bit_number)
    return lax.psum(partials, "tensor")


def adasum_pair(mine, other, section, replica):
    upper_side = jnp.right_shift(replica, section) % 2 == 1
    mine_norm = jnp.sum(mine * mine)
    other_norm = jnp.sum(other * other)
    lower_norm = jnp.where(upper_side, other_norm, mine_norm)
    upper_norm = jnp.where(upper_side, mine_norm, other_norm)
    partials = jnp.stack([jnp.sum(mine * other), lower_norm, upper_norm])
    totals = group_totals(partials, section)
    lower_coef = 1.0 - totals[0] / (2.0 * (totals[1] + epsilon))
    upper_coef = 1.0 - totals[0] / (2.0 * (totals[2] + epsilon))
    mine_coef = jnp.where(upper_side, upper_coef, lower_coef)
    other_coef = jnp.where(upper_side, lower_coef, upper_coef)
    return mine_coef * mine + other_coef * other


def by_halving(activations, out_grads):
    replicas = lax.axis_size("dp")
    section_count = replicas.bit_length() - 1
    replica = lax.axis_index("dp")
    columns = out_grads.shape[1]
    slab_rows = activations.shape[1]
    block_rows = slab_rows * lax.axis_size("tensor") // replicas
    full_grad = jnp.einsum(
        "tk,tf->kf",
        lax.all_gather(activations, "tensor", axis=1, tiled=True),
        out_grads,
        preferred_element_type=jnp.float32,
    )
    holding = full_grad.reshape(replicas, block_rows, columns)
    for section in range(section_count):
        section_bit = jnp.right_shift(replica, section) % 2
        paired = holding.reshape(-1, 2, block_rows, columns)
        keeping = lax.dynamic_index_in_dim(paired, section_bit, axis=1, keepdims=False)
        sending = lax.dynamic_index_in_dim(paired, 1 - section_bit, axis=1, keepdims=False)
        received = swapped(sending, "dp", section)
        holding = adasum_pair(keeping, received, section, replica)
    return holding.reshape(block_rows, columns)


def pair_list(count):
    return [(a, b) for a in range(count) for b in range(a, count)]


def tree_weights(gram, count):
    weights = [[(r, None)] for r in range(count)]
    while count > 1:
        half = count // 2
        low, high = [], []
        for i in range(half):
            aa, bb, ab = gram[2 * i, 2 * i], gram[2 * i + 1, 2 * i + 1], gram[2 * i, 2 * i + 1]
            bound = jnp.sqrt(aa) * jnp.sqrt(bb)
            ab = jnp.clip(ab, -bound, bound)
            low.append(1.0 - ab / (2.0 * (aa + epsilon)))
            high.append(1.0 - ab / (2.0 * (bb + epsilon)))
        merged = {}
        for i, j in pair_list(half):
            cross = gram[2 * i, 2 * j + 1]
            back = gram[2 * i + 1, 2 * j] if i != j else cross
            value = (
                low[i] * (low[j] * gram[2 * i, 2 * j] + high[j] * cross)
                + high[i] * (low[j] * back + high[j] * gram[2 * i + 1, 2 * j + 1])
            )
            merged[i, j] = jnp.maximum(value, 0.0) if i == j else value
        weights = [
            [(r, low[i] if w is None else w * low[i]) for r, w in weights[2 * i]]
            + [(r, high[i] if w is None else w * high[i]) for r, w in weights[2 * i + 1]]
            for i in range(half)
        ]
        gram, count = merged, half
    return [w for _, w in sorted(weights[0], key=lambda item: item[0])]


def kernel(
    R, Z, x_ref, y_ref, out_ref, fw, held_over,
    xg, yg, grads, part, first, second,
    zsend, zrecv, xsend, xrecv, ysend, yrecv, fsend, lsem, rrecv, rsend,
    asend, arecv, bsend, brecv,
):
    me = lax.axis_index("dp")
    z = lax.axis_index("tensor")
    chips = R // 2
    chip, core = me // 2, me % 2
    sibling = chip * 2 + 1 - core
    width = xg.shape[1]
    rows = width // CHUNKS

    def across(c, way):
        return (c // 2) * 2 + 1 - c % 2 if way == 0 else (1 - c // 2) * 2 + c % 2

    side, above = across(chip, 0), across(chip, 1)
    opposite = across(side, 1)
    via = jnp.where(core == 0, side, above)
    other = jnp.where(core == 0, above, side)
    columns = yg.shape[2]

    barrier = pltpu.get_barrier_semaphore()
    for j in range(1, Z):
        pl.semaphore_signal(barrier, inc=1, device_id=(me, (z + j) % Z), device_id_type=MESH)
    for j in range(1, R):
        pl.semaphore_signal(barrier, inc=1, device_id=((me + j) % R, z), device_id_type=MESH)
    pl.semaphore_wait(barrier, Z + R - 2)

    def remote(src, dst, send, recv, device):
        return pltpu.make_async_remote_copy(
            src_ref=src, dst_ref=dst, send_sem=send, recv_sem=recv,
            device_id=device, device_id_type=MESH,
        )

    def span(i):
        return pl.ds(pl.multiple_of(i * rows, rows), rows)

    def z_copy(src, s, i, way):
        to = z + 1 if way == 0 else z - 1
        return remote(
            src, fw.at[s, :, span(i)], zsend.at[way, s, i], zrecv.at[s, i], (me, to)
        )

    def own(i):
        return x_ref.at[:, span(i)]

    def held(s, i):
        return fw.at[s, :, span(i)]

    def go(copy, start):
        if start:
            copy.start()
        else:
            copy.wait_send()

    def scatter(src, s, i, start):
        @pl.when(s == opposite)
        def _():
            go(
                remote(
                    src, held_over.at[:, span(i)], xsend.at[s, i, 0], rrecv.at[i],
                    (2 * via + core, z),
                ),
                start,
            )

        @pl.when(s != opposite)
        def _():
            for h in range(2):
                dest = 2 * s + h
                piece = src.at[h]

                @pl.when(dest == me)
                def _():
                    if start:
                        pltpu.make_async_copy(piece, xg.at[me, span(i)], xrecv.at[me, i]).start()

                @pl.when(dest != me)
                def _():
                    go(
                        remote(
                            piece, xg.at[me, span(i)], xsend.at[s, i, h], xrecv.at[me, i],
                            (dest, z),
                        ),
                        start,
                    )

    def relay(i, start):
        r = 2 * via + core
        here = held_over.at[:, span(i)]
        if start:
            remote(here, here, rsend.at[i, 0], rrecv.at[i], (r, z)).wait_recv()
        for h in range(2):
            go(
                remote(
                    held_over.at[h, span(i)], xg.at[r, span(i)], rsend.at[i, h], xrecv.at[r, i],
                    (2 * other + h, z),
                ),
                start,
            )

    def relay_after(t, i):
        @pl.when((z - other == t) | (other - z == t))
        def _():
            relay(i, True)

    def move_along(start):
        @pl.loop(0, CHUNKS)
        def _(i):
            for way, there in ((0, z < Z - 1), (1, z > 0)):
                @pl.when(there)
                def _():
                    copy = z_copy(own(i), z, i, way)
                    if start:
                        copy.start()
                    else:
                        copy.wait_send()
            scatter(own(i), z, i, start)

        if start:
            send_out_grads()

        for t in range(1, Z):
            @pl.loop(0, CHUNKS)
            def _(i):
                for way, s, exists, further in (
                    (0, z - t, z - t >= 0, z < Z - 1),
                    (1, z + t, z + t < Z, z > 0),
                ):
                    @pl.when(exists)
                    def _():
                        if start:
                            z_copy(held(s, i), s, i, way).wait_recv()

                        @pl.when(further)
                        def _():
                            copy = z_copy(held(s, i), s, i, way)
                            if start:
                                copy.start()
                            else:
                                copy.wait_send()
                        scatter(held(s, i), s, i, start)

                if start:
                    relay_after(t - 1, i)
                if start and t == Z - 1:
                    @pl.when(i >= LAG)
                    def _():
                        relay_after(t, i - LAG)

                    @pl.when(i == CHUNKS // 2)
                    def _():
                        share_out_grads()


    def y_copy(j):
        return remote(
            y_ref, yg.at[me], ysend.at[j], yrecv.at[me], (((chip + j) % chips) * 2 + core, z)
        )

    def sibling_copy():
        return remote(y_ref, yg.at[me], ysend.at[0], yrecv.at[me], (sibling, z))

    def share_copy(j):
        r = ((chip + j) % chips) * 2 + core
        return remote(yg.at[r], yg.at[r], fsend.at[j], yrecv.at[r], (sibling, z))

    def local_y():
        return pltpu.make_async_copy(y_ref, yg.at[me], lsem)

    def send_out_grads():
        for j in range(1, chips):
            y_copy(j).start()
        sibling_copy().start()
        local_y().start()

    def share_out_grads():
        for j in range(1, chips):
            r = ((chip + j) % chips) * 2 + core
            remote(yg.at[r], yg.at[r], fsend.at[j], yrecv.at[r], (sibling, z)).wait_recv()
            share_copy(j).start()

    move_along(True)
    for f in range(LAG):
        relay_after(Z - 1, CHUNKS - LAG + f)

    local_y().wait()
    for j in range(chips):
        r = ((chip + j) % chips) * 2 + 1 - core
        remote(yg.at[r], yg.at[r], fsend.at[j], yrecv.at[r], (sibling, z)).wait_recv()

    tile = 256

    pairs = pair_list(R)

    def accumulate(b, sums):
        at = pl.ds(pl.multiple_of(b * 8, 8), 8)
        sums = list(sums)
        for q in range(columns // 128):
            blocks = [grads[r, at, pl.ds(q * 128, 128)] for r in range(R)]
            for n, (a, c) in enumerate(pairs):
                sums[n] = sums[n] + blocks[a] * blocks[c]
        return tuple(sums)

    def products(u):
        @pl.loop(0, R)
        def _(r):
            for f in range(FOLD):
                i = u * FOLD + f
                pltpu.make_async_copy(xg.at[r, span(i)], xg.at[r, span(i)], xrecv.at[r, i]).wait()

            block = pl.ds(u * FOLD * rows, FOLD * rows)

            @pl.loop(0, columns // tile)
            def _(q):
                at = pl.ds(pl.multiple_of(q * tile, tile), tile)
                grads[r, block, at] = jnp.dot(
                    xg[r, block, :], yg[r, :, at], preferred_element_type=jnp.float32
                )

    sums = tuple(jnp.zeros((8, 128), jnp.float32) for _ in pairs)
    bands = FOLD * rows // 8
    for u in range(CHUNKS // FOLD):
        products(u)
        sums = lax.fori_loop(u * bands, (u + 1) * bands, accumulate, sums)
    part[0] = jnp.zeros(part.shape[1:], jnp.float32)
    for n in range(len(pairs)):
        part[0, pl.ds(n, 1), :] = jnp.sum(sums[n], axis=0, keepdims=True)

    def around_z(j):
        return remote(part.at[0], first.at[j - 1], asend.at[j - 1], arecv.at[j - 1], (me, (z + j) % Z))

    def around_plane(j):
        return remote(
            part.at[1], second.at[j - 1], bsend.at[j - 1], brecv.at[j - 1], ((me + j) % R, z)
        )

    for j in range(1, Z):
        around_z(j).start()
    for j in range(1, Z):
        around_z(j).wait_recv()
    part[1] = part[0] + sum(first[j - 1] for j in range(1, Z))
    for j in range(1, R):
        around_plane(j).start()
    for j in range(1, R):
        around_plane(j).wait_recv()
    totals = part[1] + sum(second[j - 1] for j in range(1, R))
    totals = jnp.sum(totals, axis=1, keepdims=True)
    gram = {pair: totals[n:n + 1, :] for n, pair in enumerate(pairs)}
    weights = tree_weights(gram, R)

    band = 16

    @pl.loop(0, width // band)
    def _(b):
        at = pl.ds(pl.multiple_of(b * band, band), band)
        total = weights[0] * grads[0, at, :]
        for r in range(1, R):
            total = total + weights[r] * grads[r, at, :]
        out_ref[at, :] = total

    move_along(False)

    @pl.loop(0, CHUNKS)
    def _(i):
        relay(i, False)

    for j in range(1, chips):
        y_copy(j).wait_send()
        share_copy(j).wait_send()
    sibling_copy().wait_send()
    for j in range(1, Z):
        around_z(j).wait_send()
    for j in range(1, R):
        around_plane(j).wait_send()


def by_tiles(R, Z, activations, out_grads):
    tokens, slab = activations.shape
    columns = out_grads.shape[1]
    width = slab * Z // R
    kept = -(-len(pair_list(R)) // 8) * 8
    dma = pltpu.SemaphoreType.DMA
    return pl.pallas_call(
        functools.partial(kernel, R, Z),
        out_shape=(
            jax.ShapeDtypeStruct((width, columns), jnp.float32),
            jax.ShapeDtypeStruct((Z, 2, width, tokens), jnp.bfloat16),
            jax.ShapeDtypeStruct((2, width, tokens), jnp.bfloat16),
        ),
        in_specs=[pl.BlockSpec(memory_space=pl.ANY)] * 2,
        out_specs=(
            pl.BlockSpec(memory_space=pltpu.VMEM),
            pl.BlockSpec(memory_space=pl.ANY),
            pl.BlockSpec(memory_space=pl.ANY),
        ),
        scratch_shapes=[
            pltpu.VMEM((R, width, tokens), jnp.bfloat16),
            pltpu.VMEM((R, tokens, columns), jnp.bfloat16),
            pltpu.VMEM((R, width, columns), jnp.float32),
            pltpu.VMEM((2, kept, 128), jnp.float32),
            pltpu.VMEM((Z - 1, kept, 128), jnp.float32),
            pltpu.VMEM((R - 1, kept, 128), jnp.float32),
            dma((2, Z, CHUNKS)),
            dma((Z, CHUNKS)),
            dma((Z, CHUNKS, 2)),
            dma((R, CHUNKS)),
            dma((R // 2,)),
            dma((R,)),
            dma((R // 2,)),
            dma,
            dma((CHUNKS,)),
            dma((CHUNKS, 2)),
            dma((Z - 1,)),
            dma((Z - 1,)),
            dma((R - 1,)),
            dma((R - 1,)),
        ],
        compiler_params=pltpu.CompilerParams(
            collective_id=0, has_side_effects=True, vmem_limit_bytes=60 * 1024 * 1024
        ),
        cost_estimate=pl.CostEstimate(
            flops=2 * R * tokens * width * columns,
            bytes_accessed=2 * R * tokens * (width + columns),
            transcendentals=0,
        ),
    )(activations.T.reshape(2, width, tokens), out_grads)[0]


def solution(mesh):
    R, Z = mesh.shape["dp"], mesh.shape["tensor"]

    def on_device(activations, out_grads):
        tokens, slab = activations.shape
        columns = out_grads.shape[1]
        width = slab * Z // R
        fits = (
            R == 8 and Z == 4 and width % 128 == 0 and columns % 256 == 0
            and tokens % 128 == 0 and width % (CHUNKS * 16) == 0
            and R * (2 * tokens * (width + columns) + 4 * width * columns) < 50 * 2**20
        )
        if fits:
            return by_tiles(R, Z, activations, out_grads)
        return by_halving(activations, out_grads)

    return jax.shard_map(
        on_device,
        mesh=mesh,
        in_specs=(P("dp", "tensor"), P("dp", "tensor")),
        out_specs=P("dp", "tensor"),
        check_vma=False,
    )
```

```python
import functools
import jax
import jax.numpy as jnp
from jax import lax
from jax.experimental import pallas as pl
from jax.experimental.pallas import tpu as pltpu
from jax.sharding import PartitionSpec as P

epsilon = 1e-06
MESH = pl.DeviceIdType.MESH
CHUNKS = 8
FOLD = 4
WINDOW = 3


def swapped(x, axis, apart):
    return lax.ppermute(x, axis, [(i, i ^ 1 << apart) for i in range(lax.axis_size(axis))])


def group_totals(partials, section):
    for bit_number in range(section + 1):
        partials = partials + swapped(partials, "dp", bit_number)
    return lax.psum(partials, "tensor")


def adasum_pair(mine, other, section, replica):
    upper_side = jnp.right_shift(replica, section) % 2 == 1
    mine_norm = jnp.sum(mine * mine)
    other_norm = jnp.sum(other * other)
    lower_norm = jnp.where(upper_side, other_norm, mine_norm)
    upper_norm = jnp.where(upper_side, mine_norm, other_norm)
    partials = jnp.stack([jnp.sum(mine * other), lower_norm, upper_norm])
    totals = group_totals(partials, section)
    lower_coef = 1.0 - totals[0] / (2.0 * (totals[1] + epsilon))
    upper_coef = 1.0 - totals[0] / (2.0 * (totals[2] + epsilon))
    mine_coef = jnp.where(upper_side, upper_coef, lower_coef)
    other_coef = jnp.where(upper_side, lower_coef, upper_coef)
    return mine_coef * mine + other_coef * other


def by_halving(activations, out_grads):
    replicas = lax.axis_size("dp")
    section_count = replicas.bit_length() - 1
    replica = lax.axis_index("dp")
    columns = out_grads.shape[1]
    slab_rows = activations.shape[1]
    block_rows = slab_rows * lax.axis_size("tensor") // replicas
    full_grad = jnp.einsum(
        "tk,tf->kf",
        lax.all_gather(activations, "tensor", axis=1, tiled=True),
        out_grads,
        preferred_element_type=jnp.float32,
    )
    holding = full_grad.reshape(replicas, block_rows, columns)
    for section in range(section_count):
        section_bit = jnp.right_shift(replica, section) % 2
        paired = holding.reshape(-1, 2, block_rows, columns)
        keeping = lax.dynamic_index_in_dim(paired, section_bit, axis=1, keepdims=False)
        sending = lax.dynamic_index_in_dim(paired, 1 - section_bit, axis=1, keepdims=False)
        received = swapped(sending, "dp", section)
        holding = adasum_pair(keeping, received, section, replica)
    return holding.reshape(block_rows, columns)


def pair_list(count):
    return [(a, b) for a in range(count) for b in range(a, count)]


def tree_weights(gram, count):
    weights = [[(r, None)] for r in range(count)]
    while count > 1:
        half = count // 2
        low, high = [], []
        for i in range(half):
            aa, bb, ab = gram[2 * i, 2 * i], gram[2 * i + 1, 2 * i + 1], gram[2 * i, 2 * i + 1]
            bound = jnp.sqrt(aa) * jnp.sqrt(bb)
            ab = jnp.clip(ab, -bound, bound)
            low.append(1.0 - ab / (2.0 * (aa + epsilon)))
            high.append(1.0 - ab / (2.0 * (bb + epsilon)))
        merged = {}
        for i, j in pair_list(half):
            cross = gram[2 * i, 2 * j + 1]
            back = gram[2 * i + 1, 2 * j] if i != j else cross
            value = (
                low[i] * (low[j] * gram[2 * i, 2 * j] + high[j] * cross)
                + high[i] * (low[j] * back + high[j] * gram[2 * i + 1, 2 * j + 1])
            )
            merged[i, j] = jnp.maximum(value, 0.0) if i == j else value
        weights = [
            [(r, low[i] if w is None else w * low[i]) for r, w in weights[2 * i]]
            + [(r, high[i] if w is None else w * high[i]) for r, w in weights[2 * i + 1]]
            for i in range(half)
        ]
        gram, count = merged, half
    return [w for _, w in sorted(weights[0], key=lambda item: item[0])]


def kernel(
    R, Z, x_ref, y_ref, out_ref, fw,
    xg, yg, grads, part, first, second,
    zsend, zrecv, xsend, xrecv, ysend, yrecv, fsend, lsem, asend, arecv, bsend, brecv,
):
    me = lax.axis_index("dp")
    z = lax.axis_index("tensor")
    chips = R // 2
    chip, core = me // 2, me % 2
    sibling = chip * 2 + 1 - core
    width = xg.shape[1]
    rows = width // CHUNKS
    columns = yg.shape[2]

    barrier = pltpu.get_barrier_semaphore()
    for j in range(1, Z):
        pl.semaphore_signal(barrier, inc=1, device_id=(me, (z + j) % Z), device_id_type=MESH)
    for j in range(1, R):
        pl.semaphore_signal(barrier, inc=1, device_id=((me + j) % R, z), device_id_type=MESH)
    pl.semaphore_wait(barrier, Z + R - 2)

    def remote(src, dst, send, recv, device):
        return pltpu.make_async_remote_copy(
            src_ref=src, dst_ref=dst, send_sem=send, recv_sem=recv,
            device_id=device, device_id_type=MESH,
        )

    def span(i):
        return pl.ds(pl.multiple_of(i * rows, rows), rows)

    def z_copy(src, s, i, way):
        to = z + 1 if way == 0 else z - 1
        return remote(
            src, fw.at[s, :, span(i)], zsend.at[way, s, i], zrecv.at[s, i], (me, to)
        )

    def own(i):
        return x_ref.at[:, span(i)]

    def held(s, i):
        return fw.at[s, :, span(i)]

    def scatter(src, s, i, start):
        for h in range(2):
            dest = 2 * s + h
            piece = src.at[h]

            @pl.when(dest == me)
            def _():
                if start:
                    pltpu.make_async_copy(piece, xg.at[me, span(i)], xrecv.at[me, i]).start()

            @pl.when(dest != me)
            def _():
                copy = remote(
                    piece, xg.at[me, span(i)], xsend.at[s, i, h], xrecv.at[me, i], (dest, z)
                )
                if start:
                    copy.start()
                else:
                    copy.wait_send()

    def move_along(start):
        @pl.loop(0, CHUNKS)
        def _(i):
            for way, there in ((0, z < Z - 1), (1, z > 0)):
                @pl.when(there)
                def _():
                    if start:
                        z_copy(own(i), z, i, way).start()

                        @pl.when(i >= WINDOW)
                        def _():
                            z_copy(own(i - WINDOW), z, i - WINDOW, way).wait_send()
                    else:
                        @pl.when(i >= CHUNKS - WINDOW)
                        def _():
                            z_copy(own(i), z, i, way).wait_send()
            scatter(own(i), z, i, start)

        if start:
            send_out_grads()

        for t in range(1, Z):
            @pl.loop(0, CHUNKS)
            def _(i):
                for way, s, exists, further in (
                    (0, z - t, z - t >= 0, z < Z - 1),
                    (1, z + t, z + t < Z, z > 0),
                ):
                    @pl.when(exists)
                    def _():
                        if start:
                            z_copy(held(s, i), s, i, way).wait_recv()

                        @pl.when(further)
                        def _():
                            copy = z_copy(held(s, i), s, i, way)
                            if start:
                                copy.start()
                            else:
                                copy.wait_send()
                        scatter(held(s, i), s, i, start)


    def y_copy(j):
        return remote(
            y_ref, yg.at[me], ysend.at[j], yrecv.at[me], (((chip + j) % chips) * 2 + core, z)
        )

    def sibling_copy():
        return remote(y_ref, yg.at[me], ysend.at[0], yrecv.at[me], (sibling, z))

    def share_copy(j):
        r = ((chip + j) % chips) * 2 + core
        return remote(yg.at[r], yg.at[r], fsend.at[j], yrecv.at[r], (sibling, z))

    def local_y():
        return pltpu.make_async_copy(y_ref, yg.at[me], lsem)

    def send_out_grads():
        for j in range(1, chips):
            y_copy(j).start()
        sibling_copy().start()
        local_y().start()

    def share_out_grads():
        for j in range(1, chips):
            r = ((chip + j) % chips) * 2 + core
            remote(yg.at[r], yg.at[r], fsend.at[j], yrecv.at[r], (sibling, z)).wait_recv()
            share_copy(j).start()

    move_along(True)
    share_out_grads()

    local_y().wait()
    for j in range(chips):
        r = ((chip + j) % chips) * 2 + 1 - core
        remote(yg.at[r], yg.at[r], fsend.at[j], yrecv.at[r], (sibling, z)).wait_recv()

    tile = 256

    @pl.loop(0, CHUNKS // FOLD)
    def _(u):
        @pl.loop(0, R)
        def _(r):
            for f in range(FOLD):
                i = u * FOLD + f
                pltpu.make_async_copy(xg.at[r, span(i)], xg.at[r, span(i)], xrecv.at[r, i]).wait()

            block = pl.ds(pl.multiple_of(u * FOLD * rows, FOLD * rows), FOLD * rows)

            @pl.loop(0, columns // tile)
            def _(q):
                at = pl.ds(pl.multiple_of(q * tile, tile), tile)
                grads[r, block, at] = jnp.dot(
                    xg[r, block, :], yg[r, :, at], preferred_element_type=jnp.float32
                )

    pairs = pair_list(R)

    def accumulate(b, sums):
        at = pl.ds(pl.multiple_of(b * 8, 8), 8)
        sums = list(sums)
        for q in range(columns // 128):
            blocks = [grads[r, at, pl.ds(q * 128, 128)] for r in range(R)]
            for n, (a, c) in enumerate(pairs):
                sums[n] = sums[n] + blocks[a] * blocks[c]
        return tuple(sums)

    sums = lax.fori_loop(
        0, width // 8, accumulate, tuple(jnp.zeros((8, 128), jnp.float32) for _ in pairs)
    )
    part[0] = jnp.zeros(part.shape[1:], jnp.float32)
    for n in range(len(pairs)):
        part[0, pl.ds(n, 1), :] = jnp.sum(sums[n], axis=0, keepdims=True)

    def around_z(j):
        return remote(part.at[0], first.at[j - 1], asend.at[j - 1], arecv.at[j - 1], (me, (z + j) % Z))

    def around_plane(j):
        return remote(
            part.at[1], second.at[j - 1], bsend.at[j - 1], brecv.at[j - 1], ((me + j) % R, z)
        )

    for j in range(1, Z):
        around_z(j).start()
    for j in range(1, Z):
        around_z(j).wait_recv()
    part[1] = part[0] + sum(first[j - 1] for j in range(1, Z))
    for j in range(1, R):
        around_plane(j).start()
    for j in range(1, R):
        around_plane(j).wait_recv()
    totals = part[1] + sum(second[j - 1] for j in range(1, R))
    totals = jnp.sum(totals, axis=1, keepdims=True)
    gram = {pair: totals[n:n + 1, :] for n, pair in enumerate(pairs)}
    weights = tree_weights(gram, R)

    band = 16

    @pl.loop(0, width // band)
    def _(b):
        at = pl.ds(pl.multiple_of(b * band, band), band)
        total = weights[0] * grads[0, at, :]
        for r in range(1, R):
            total = total + weights[r] * grads[r, at, :]
        out_ref[at, :] = total

    move_along(False)
    for j in range(1, chips):
        y_copy(j).wait_send()
        share_copy(j).wait_send()
    sibling_copy().wait_send()
    for j in range(1, Z):
        around_z(j).wait_send()
    for j in range(1, R):
        around_plane(j).wait_send()


def by_tiles(R, Z, activations, out_grads):
    tokens, slab = activations.shape
    columns = out_grads.shape[1]
    width = slab * Z // R
    kept = -(-len(pair_list(R)) // 8) * 8
    dma = pltpu.SemaphoreType.DMA
    return pl.pallas_call(
        functools.partial(kernel, R, Z),
        out_shape=(
            jax.ShapeDtypeStruct((width, columns), jnp.float32),
            jax.ShapeDtypeStruct((Z, 2, width, tokens), jnp.bfloat16),
        ),
        in_specs=[pl.BlockSpec(memory_space=pl.ANY)] * 2,
        out_specs=(
            pl.BlockSpec(memory_space=pltpu.VMEM),
            pl.BlockSpec(memory_space=pl.ANY),
        ),
        scratch_shapes=[
            pltpu.VMEM((R, width, tokens), jnp.bfloat16),
            pltpu.VMEM((R, tokens, columns), jnp.bfloat16),
            pltpu.VMEM((R, width, columns), jnp.float32),
            pltpu.VMEM((2, kept, 128), jnp.float32),
            pltpu.VMEM((Z - 1, kept, 128), jnp.float32),
            pltpu.VMEM((R - 1, kept, 128), jnp.float32),
            dma((2, Z, CHUNKS)),
            dma((Z, CHUNKS)),
            dma((Z, CHUNKS, 2)),
            dma((R, CHUNKS)),
            dma((R // 2,)),
            dma((R,)),
            dma((R // 2,)),
            dma,
            dma((Z - 1,)),
            dma((Z - 1,)),
            dma((R - 1,)),
            dma((R - 1,)),
        ],
        compiler_params=pltpu.CompilerParams(
            collective_id=0, has_side_effects=True, vmem_limit_bytes=60 * 1024 * 1024
        ),
        cost_estimate=pl.CostEstimate(
            flops=2 * R * tokens * width * columns,
            bytes_accessed=2 * R * tokens * (width + columns),
            transcendentals=0,
        ),
    )(activations.T.reshape(2, width, tokens), out_grads)[0]


def solution(mesh):
    R, Z = mesh.shape["dp"], mesh.shape["tensor"]

    def on_device(activations, out_grads):
        tokens, slab = activations.shape
        columns = out_grads.shape[1]
        width = slab * Z // R
        fits = (
            R == 8 and Z == 4 and width % 128 == 0 and columns % 256 == 0
            and tokens % 128 == 0 and width % (CHUNKS * 16) == 0
            and R * (2 * tokens * (width + columns) + 4 * width * columns) < 50 * 2**20
        )
        if fits:
            return by_tiles(R, Z, activations, out_grads)
        return by_halving(activations, out_grads)

    return jax.shard_map(
        on_device,
        mesh=mesh,
        in_specs=(P("dp", "tensor"), P("dp", "tensor")),
        out_specs=P("dp", "tensor"),
        check_vma=False,
    )
```

```python
import functools
import jax
import jax.numpy as jnp
from jax import lax
from jax.experimental import pallas as pl
from jax.experimental.pallas import tpu as pltpu
from jax.sharding import PartitionSpec as P

epsilon = 1e-06
MESH = pl.DeviceIdType.MESH
CHUNKS = 4
FOLD = 2


def swapped(x, axis, apart):
    return lax.ppermute(x, axis, [(i, i ^ 1 << apart) for i in range(lax.axis_size(axis))])


def group_totals(partials, section):
    for bit_number in range(section + 1):
        partials = partials + swapped(partials, "dp", bit_number)
    return lax.psum(partials, "tensor")


def adasum_pair(mine, other, section, replica):
    upper_side = jnp.right_shift(replica, section) % 2 == 1
    mine_norm = jnp.sum(mine * mine)
    other_norm = jnp.sum(other * other)
    lower_norm = jnp.where(upper_side, other_norm, mine_norm)
    upper_norm = jnp.where(upper_side, mine_norm, other_norm)
    partials = jnp.stack([jnp.sum(mine * other), lower_norm, upper_norm])
    totals = group_totals(partials, section)
    lower_coef = 1.0 - totals[0] / (2.0 * (totals[1] + epsilon))
    upper_coef = 1.0 - totals[0] / (2.0 * (totals[2] + epsilon))
    mine_coef = jnp.where(upper_side, upper_coef, lower_coef)
    other_coef = jnp.where(upper_side, lower_coef, upper_coef)
    return mine_coef * mine + other_coef * other


def by_halving(activations, out_grads):
    replicas = lax.axis_size("dp")
    section_count = replicas.bit_length() - 1
    replica = lax.axis_index("dp")
    columns = out_grads.shape[1]
    slab_rows = activations.shape[1]
    block_rows = slab_rows * lax.axis_size("tensor") // replicas
    full_grad = jnp.einsum(
        "tk,tf->kf",
        lax.all_gather(activations, "tensor", axis=1, tiled=True),
        out_grads,
        preferred_element_type=jnp.float32,
    )
    holding = full_grad.reshape(replicas, block_rows, columns)
    for section in range(section_count):
        section_bit = jnp.right_shift(replica, section) % 2
        paired = holding.reshape(-1, 2, block_rows, columns)
        keeping = lax.dynamic_index_in_dim(paired, section_bit, axis=1, keepdims=False)
        sending = lax.dynamic_index_in_dim(paired, 1 - section_bit, axis=1, keepdims=False)
        received = swapped(sending, "dp", section)
        holding = adasum_pair(keeping, received, section, replica)
    return holding.reshape(block_rows, columns)


def pair_list(count):
    return [(a, b) for a in range(count) for b in range(a, count)]


def tree_weights(gram, count):
    weights = [[(r, None)] for r in range(count)]
    while count > 1:
        half = count // 2
        low, high = [], []
        for i in range(half):
            aa, bb, ab = gram[2 * i, 2 * i], gram[2 * i + 1, 2 * i + 1], gram[2 * i, 2 * i + 1]
            bound = jnp.sqrt(aa) * jnp.sqrt(bb)
            ab = jnp.clip(ab, -bound, bound)
            low.append(1.0 - ab / (2.0 * (aa + epsilon)))
            high.append(1.0 - ab / (2.0 * (bb + epsilon)))
        merged = {}
        for i, j in pair_list(half):
            cross = gram[2 * i, 2 * j + 1]
            back = gram[2 * i + 1, 2 * j] if i != j else cross
            value = (
                low[i] * (low[j] * gram[2 * i, 2 * j] + high[j] * cross)
                + high[i] * (low[j] * back + high[j] * gram[2 * i + 1, 2 * j + 1])
            )
            merged[i, j] = jnp.maximum(value, 0.0) if i == j else value
        weights = [
            [(r, low[i] if w is None else w * low[i]) for r, w in weights[2 * i]]
            + [(r, high[i] if w is None else w * high[i]) for r, w in weights[2 * i + 1]]
            for i in range(half)
        ]
        gram, count = merged, half
    return [w for _, w in sorted(weights[0], key=lambda item: item[0])]


def kernel(
    R, Z, x_ref, y_ref, out_ref, fw,
    xg, yg, grads, part, first, second,
    zsend, zrecv, xsend, xrecv, ysend, yrecv, fsend, lsem, asend, arecv, bsend, brecv,
):
    me = lax.axis_index("dp")
    z = lax.axis_index("tensor")
    chips = R // 2
    chip, core = me // 2, me % 2
    sibling = chip * 2 + 1 - core
    width = xg.shape[1]
    rows = width // CHUNKS
    columns = yg.shape[2]

    barrier = pltpu.get_barrier_semaphore()
    for j in range(1, Z):
        pl.semaphore_signal(barrier, inc=1, device_id=(me, (z + j) % Z), device_id_type=MESH)
    for j in range(1, R):
        pl.semaphore_signal(barrier, inc=1, device_id=((me + j) % R, z), device_id_type=MESH)
    pl.semaphore_wait(barrier, Z + R - 2)

    def remote(src, dst, send, recv, device):
        return pltpu.make_async_remote_copy(
            src_ref=src, dst_ref=dst, send_sem=send, recv_sem=recv,
            device_id=device, device_id_type=MESH,
        )

    def span(i):
        return pl.ds(pl.multiple_of(i * rows, rows), rows)

    def z_copy(src, s, i, way):
        to = z + 1 if way == 0 else z - 1
        return remote(
            src, fw.at[s, :, span(i)], zsend.at[way, s, i], zrecv.at[s, i], (me, to)
        )

    def own(i):
        return x_ref.at[:, span(i)]

    def held(s, i):
        return fw.at[s, :, span(i)]

    def scatter(src, s, i, start):
        for h in range(2):
            dest = 2 * s + h
            piece = src.at[h]

            @pl.when(dest == me)
            def _():
                if start:
                    pltpu.make_async_copy(piece, xg.at[me, span(i)], xrecv.at[me, i]).start()

            @pl.when(dest != me)
            def _():
                copy = remote(
                    piece, xg.at[me, span(i)], xsend.at[s, i, h], xrecv.at[me, i], (dest, z)
                )
                if start:
                    copy.start()
                else:
                    copy.wait_send()

    def move_along(start):
        @pl.loop(0, CHUNKS)
        def _(i):
            for way, there in ((0, z < Z - 1), (1, z > 0)):
                @pl.when(there)
                def _():
                    copy = z_copy(own(i), z, i, way)
                    if start:
                        copy.start()
                    else:
                        copy.wait_send()
            scatter(own(i), z, i, start)

        if start:
            send_out_grads()

        for t in range(1, Z):
            @pl.loop(0, CHUNKS)
            def _(i):
                for way, s, exists, further in (
                    (0, z - t, z - t >= 0, z < Z - 1),
                    (1, z + t, z + t < Z, z > 0),
                ):
                    @pl.when(exists)
                    def _():
                        if start:
                            z_copy(held(s, i), s, i, way).wait_recv()

                        @pl.when(further)
                        def _():
                            copy = z_copy(held(s, i), s, i, way)
                            if start:
                                copy.start()
                            else:
                                copy.wait_send()
                        scatter(held(s, i), s, i, start)


    def y_copy(j):
        return remote(
            y_ref, yg.at[me], ysend.at[j], yrecv.at[me], (((chip + j) % chips) * 2 + core, z)
        )

    def sibling_copy():
        return remote(y_ref, yg.at[me], ysend.at[0], yrecv.at[me], (sibling, z))

    def share_copy(j):
        r = ((chip + j) % chips) * 2 + core
        return remote(yg.at[r], yg.at[r], fsend.at[j], yrecv.at[r], (sibling, z))

    def local_y():
        return pltpu.make_async_copy(y_ref, yg.at[me], lsem)

    def send_out_grads():
        for j in range(1, chips):
            y_copy(j).start()
        sibling_copy().start()
        local_y().start()

    def share_out_grads():
        for j in range(1, chips):
            r = ((chip + j) % chips) * 2 + core
            remote(yg.at[r], yg.at[r], fsend.at[j], yrecv.at[r], (sibling, z)).wait_recv()
            share_copy(j).start()

    move_along(True)
    share_out_grads()

    local_y().wait()
    for j in range(chips):
        r = ((chip + j) % chips) * 2 + 1 - core
        remote(yg.at[r], yg.at[r], fsend.at[j], yrecv.at[r], (sibling, z)).wait_recv()

    tile = 256

    @pl.loop(0, CHUNKS // FOLD)
    def _(u):
        @pl.loop(0, R)
        def _(r):
            for f in range(FOLD):
                i = u * FOLD + f
                pltpu.make_async_copy(xg.at[r, span(i)], xg.at[r, span(i)], xrecv.at[r, i]).wait()

            block = pl.ds(pl.multiple_of(u * FOLD * rows, FOLD * rows), FOLD * rows)

            @pl.loop(0, columns // tile)
            def _(q):
                at = pl.ds(pl.multiple_of(q * tile, tile), tile)
                grads[r, block, at] = jnp.dot(
                    xg[r, block, :], yg[r, :, at], preferred_element_type=jnp.float32
                )

    pairs = pair_list(R)

    def accumulate(b, sums):
        at = pl.ds(pl.multiple_of(b * 8, 8), 8)
        sums = list(sums)
        for q in range(columns // 128):
            blocks = [grads[r, at, pl.ds(q * 128, 128)] for r in range(R)]
            for n, (a, c) in enumerate(pairs):
                sums[n] = sums[n] + blocks[a] * blocks[c]
        return tuple(sums)

    sums = lax.fori_loop(
        0, width // 8, accumulate, tuple(jnp.zeros((8, 128), jnp.float32) for _ in pairs)
    )
    part[0] = jnp.zeros(part.shape[1:], jnp.float32)
    for n in range(len(pairs)):
        part[0, pl.ds(n, 1), :] = jnp.sum(sums[n], axis=0, keepdims=True)

    def around_z(j):
        return remote(part.at[0], first.at[j - 1], asend.at[j - 1], arecv.at[j - 1], (me, (z + j) % Z))

    def around_plane(j):
        return remote(
            part.at[1], second.at[j - 1], bsend.at[j - 1], brecv.at[j - 1], ((me + j) % R, z)
        )

    for j in range(1, Z):
        around_z(j).start()
    for j in range(1, Z):
        around_z(j).wait_recv()
    part[1] = part[0] + sum(first[j - 1] for j in range(1, Z))
    for j in range(1, R):
        around_plane(j).start()
    for j in range(1, R):
        around_plane(j).wait_recv()
    totals = part[1] + sum(second[j - 1] for j in range(1, R))
    totals = jnp.sum(totals, axis=1, keepdims=True)
    gram = {pair: totals[n:n + 1, :] for n, pair in enumerate(pairs)}
    weights = tree_weights(gram, R)

    band = 16

    @pl.loop(0, width // band)
    def _(b):
        at = pl.ds(pl.multiple_of(b * band, band), band)
        total = weights[0] * grads[0, at, :]
        for r in range(1, R):
            total = total + weights[r] * grads[r, at, :]
        out_ref[at, :] = total

    move_along(False)
    for j in range(1, chips):
        y_copy(j).wait_send()
        share_copy(j).wait_send()
    sibling_copy().wait_send()
    for j in range(1, Z):
        around_z(j).wait_send()
    for j in range(1, R):
        around_plane(j).wait_send()


def by_tiles(R, Z, activations, out_grads):
    tokens, slab = activations.shape
    columns = out_grads.shape[1]
    width = slab * Z // R
    kept = -(-len(pair_list(R)) // 8) * 8
    dma = pltpu.SemaphoreType.DMA
    return pl.pallas_call(
        functools.partial(kernel, R, Z),
        out_shape=(
            jax.ShapeDtypeStruct((width, columns), jnp.float32),
            jax.ShapeDtypeStruct((Z, 2, width, tokens), jnp.bfloat16),
        ),
        in_specs=[pl.BlockSpec(memory_space=pl.ANY)] * 2,
        out_specs=(
            pl.BlockSpec(memory_space=pltpu.VMEM),
            pl.BlockSpec(memory_space=pl.ANY),
        ),
        scratch_shapes=[
            pltpu.VMEM((R, width, tokens), jnp.bfloat16),
            pltpu.VMEM((R, tokens, columns), jnp.bfloat16),
            pltpu.VMEM((R, width, columns), jnp.float32),
            pltpu.VMEM((2, kept, 128), jnp.float32),
            pltpu.VMEM((Z - 1, kept, 128), jnp.float32),
            pltpu.VMEM((R - 1, kept, 128), jnp.float32),
            dma((2, Z, CHUNKS)),
            dma((Z, CHUNKS)),
            dma((Z, CHUNKS, 2)),
            dma((R, CHUNKS)),
            dma((R // 2,)),
            dma((R,)),
            dma((R // 2,)),
            dma,
            dma((Z - 1,)),
            dma((Z - 1,)),
            dma((R - 1,)),
            dma((R - 1,)),
        ],
        compiler_params=pltpu.CompilerParams(
            collective_id=0, has_side_effects=True, vmem_limit_bytes=60 * 1024 * 1024
        ),
        cost_estimate=pl.CostEstimate(
            flops=2 * R * tokens * width * columns,
            bytes_accessed=2 * R * tokens * (width + columns),
            transcendentals=0,
        ),
    )(activations.T.reshape(2, width, tokens), out_grads)[0]


def solution(mesh):
    R, Z = mesh.shape["dp"], mesh.shape["tensor"]

    def on_device(activations, out_grads):
        tokens, slab = activations.shape
        columns = out_grads.shape[1]
        width = slab * Z // R
        fits = (
            R == 8 and Z == 4 and width % 128 == 0 and columns % 256 == 0
            and tokens % 128 == 0 and width % (CHUNKS * 16) == 0
            and R * (2 * tokens * (width + columns) + 4 * width * columns) < 50 * 2**20
        )
        if fits:
            return by_tiles(R, Z, activations, out_grads)
        return by_halving(activations, out_grads)

    return jax.shard_map(
        on_device,
        mesh=mesh,
        in_specs=(P("dp", "tensor"), P("dp", "tensor")),
        out_specs=P("dp", "tensor"),
        check_vma=False,
    )
```
